512 devices in a mesh: row: 64 (over z, y), blk: 8 (over x, core).
Axes of the slice: x: 4, y: 8, z: 8, core: 2. Of those that a mesh axis runs over, the one named last changes fastest.
Arguments:
- matrix: float32 [65536, 2048], P('row', 'blk'), may hold values from -24 to 24, as said below
- sender_slot: int32 [4, 8], P(None, 'blk'), may hold values from 0 to 1
Outputs:
- rotated_matrix: float32 [65536, 2048], P('row', 'blk')
The draws below stay inside these ranges and needn't reach their ends.
Inputs may be any that keep to these rules, and one draw needn't show every extreme that they name: Each entry of the matrix has a column factor that differs from column to column.
All inputs are finite; a program needn't handle non-finite values.
Results may differ from the reference program's by a relative error of at most 0.0003.
Values sent between devices are 32-bit elements; how exact they have to be, the bound alone decides.
No kernel may reach another device: no remote copies, remote signals or barrier semaphores. Data moves between devices by JAX's collectives and lax.ppermute only.
A program may use at most 64 MiB of HBM per device.

```python
import jax
import jax.numpy as jnp
from jax import lax

BLOCK = 128
STEPS = 4
ROUNDS = 8
ROWS = 65536
COLS = 2048
N_BLK = 8


def draw_matrix(key, part):
    key = jax.random.fold_in(key, 11)
    noise_key, row_key, column_key = jax.random.split(key, 3)
    row_scale = jnp.exp(jax.random.uniform(row_key, (ROWS, 1), jnp.float32, jnp.log(0.5), jnp.log(2.0)))
    column_scale = jnp.exp(jax.random.uniform(column_key, (1, COLS), jnp.float32, jnp.log(0.3), jnp.log(3.0)))
    noise = jnp.clip(jax.random.normal(noise_key, (ROWS, COLS), jnp.float32), -4.0, 4.0)
    values = noise * row_scale * column_scale
    return values


def with_ends(drawn, stream_key, low, largest):
    dims = drawn.shape
    place = [jax.random.randint(jax.random.fold_in(stream_key, axis), (), 0, dims[axis]) for axis in range(len(dims))]
    drawn = drawn.at[tuple(place)].set(low)
    longest = dims.index(max(dims))
    place[longest] = (place[longest] + 1) % dims[longest]
    return drawn.at[tuple(place)].set(largest)


def setup_inputs(seed: int = 0) -> dict:
    streams_of = jax.random.split(jax.random.key(seed), 3)
    matrix = draw_matrix(jax.random.fold_in(streams_of[2], 71), 0)
    sender_slot = with_ends(jax.random.randint(streams_of[1], (STEPS, N_BLK), 0, 2), jax.random.fold_in(streams_of[1], 1), 0, 1).astype(jnp.int32)
    return {"matrix": matrix, "sender_slot": sender_slot}


def partners(round_index, dimension):
    position = jnp.arange(dimension, dtype=jnp.int32)
    period = dimension - 1
    opposite = jnp.mod(2 * round_index - position, period)
    partner = jnp.where(opposite == position, period, opposite)
    return jnp.where(position == period, jnp.mod(round_index, period), partner).astype(jnp.int32)


def jacobi_rounds(gram_matrix, offset):
    dimension = gram_matrix.shape[0]
    position = jnp.arange(dimension, dtype=jnp.int32)

    def one_round(round_index, carried):
        current, rotation = carried
        partner = partners(offset + round_index, dimension)
        is_lower = position < partner
        low_index = jnp.where(is_lower, position, partner)
        high_index = jnp.where(is_lower, partner, position)
        diagonal_values = jnp.diagonal(current)
        coupling = current[low_index, high_index]
        difference = diagonal_values[high_index] - diagonal_values[low_index]
        sign_term = jnp.where(difference >= 0.0, 1.0, -1.0)
        rotation_angle = 0.5 * jnp.arctan2(2.0 * sign_term * coupling, jnp.abs(difference))
        cosine_term = jnp.cos(rotation_angle)
        sine_term = jnp.where(is_lower, -1.0, 1.0) * jnp.sin(rotation_angle)
        half_turned = current * cosine_term[None, :] + jnp.take(current, partner, axis=1) * sine_term[None, :]
        current = cosine_term[:, None] * half_turned + sine_term[:, None] * jnp.take(half_turned, partner, axis=0)
        rotation = rotation * cosine_term[None, :] + jnp.take(rotation, partner, axis=1) * sine_term[None, :]
        return current, rotation

    identity = jnp.eye(dimension, dtype=jnp.float32)
    return lax.fori_loop(0, ROUNDS, one_round, (gram_matrix, identity))


def reference(matrix, sender_slot):
    row_count = matrix.shape[0]
    pair_blocks = matrix.reshape(row_count, N_BLK, 2 * BLOCK).transpose(1, 0, 2)
    for step_index in range(STEPS):
        gram_blocks = jnp.einsum("krp,krq->kpq", pair_blocks, pair_blocks, precision=lax.Precision.HIGHEST)
        offset = step_index * ROUNDS
        finals, rotations = jax.vmap(lambda single: jacobi_rounds(single, offset))(gram_blocks)
        rotated = jnp.einsum("krp,kpq->krq", pair_blocks, rotations, precision=lax.Precision.HIGHEST)
        chosen = (sender_slot[step_index] == 1)[:, None, None]
        first_half = rotated[:, :, :BLOCK]
        second_half = rotated[:, :, BLOCK:]
        moved_cols = jnp.where(chosen, second_half, first_half)
        kept_cols = jnp.where(chosen, first_half, second_half)
        pair_blocks = jnp.concatenate([kept_cols, jnp.roll(moved_cols, 1, axis=0)], axis=2)
    return pair_blocks.transpose(1, 0, 2).reshape(row_count, N_BLK * 2 * BLOCK)
```

```python
import functools

import jax
import jax.numpy as jnp
from jax import lax
from jax.experimental import pallas as pl
from jax.experimental.pallas import tpu as pltpu
from jax.sharding import PartitionSpec as P

STEPS = 4
ROUNDS = 8
N = 256
HALF = 128
PERIOD = N - 1


def dot(left, right, over=(1, 0)):
    return lax.dot_general(
        left,
        right,
        (((over[0],), (over[1],)), ((), ())),
        precision=lax.Precision.HIGHEST,
        preferred_element_type=jnp.float32,
    )


def seats(position, round_index):
    upper = position + round_index
    upper = jnp.where(upper >= PERIOD, upper - PERIOD, upper)
    lower = round_index - (position - HALF)
    lower = jnp.where(lower < 0, lower + PERIOD, lower)
    return jnp.where(position < HALF, upper, jnp.where(position == HALF, PERIOD, lower))


def placing(round_index):
    index = lax.broadcasted_iota(jnp.int32, (N, N), 0)
    position = lax.broadcasted_iota(jnp.int32, (N, N), 1)
    return (index == seats(position, round_index)).astype(jnp.float32)


def rotations(upper_diag, coupling, lower_diag, round_index):
    position = lax.broadcasted_iota(jnp.int32, (1, HALF), 1)
    is_lower = seats(position, round_index) < seats(position + HALF, round_index)
    difference = jnp.where(is_lower, lower_diag - upper_diag, upper_diag - lower_diag)
    x = jnp.abs(difference)
    y = jnp.where(difference >= 0.0, 2.0 * coupling, -2.0 * coupling)
    largest = jnp.maximum(x, jnp.abs(y))
    scale = jnp.where(largest > 0.0, largest, 1.0)
    x = jnp.where(largest > 0.0, x / scale, 1.0)
    y = y / scale
    tangent = y / (x + jnp.sqrt(x * x + y * y))
    cosine = 1.0 / jnp.sqrt(1.0 + tangent * tangent)
    sine = tangent * cosine
    return cosine, jnp.where(is_lower, -sine, sine)


def turn(upper, lower, cosine, sine):
    return cosine * upper + sine * lower, cosine * lower - sine * upper


def shift(upper, lower, axis):
    at = lax.broadcasted_iota(jnp.int32, upper.shape, axis)
    new_upper = jnp.where(at == HALF - 1, lower, pltpu.roll(upper, HALF - 1, axis))
    moved = pltpu.roll(jnp.where(at == 0, upper, lower), 1, axis)
    return new_upper, jnp.where(at == 0, lower, moved)


def jacobi(gram, offset, parts):
    uu, ul, lu, ll, qu, ql = parts
    start = placing(offset)
    laid_out = dot(start, dot(gram, start), (0, 0))
    uu[...] = laid_out[:HALF, :HALF]
    ul[...] = laid_out[:HALF, HALF:]
    lu[...] = laid_out[HALF:, :HALF]
    ll[...] = laid_out[HALF:, HALF:]
    qu[...] = start[:, :HALF]
    ql[...] = start[:, HALF:]
    shape = (HALF, HALF)
    eye = lax.broadcasted_iota(jnp.int32, shape, 0) == lax.broadcasted_iota(jnp.int32, shape, 1)

    def diagonal(ref):
        return jnp.sum(jnp.where(eye, ref[...], 0.0), axis=0, keepdims=True)

    def stood(row):
        return jnp.sum(jnp.where(eye, jnp.broadcast_to(row, shape), 0.0), axis=1, keepdims=True)

    for round_index in range(offset, offset + ROUNDS):
        cosine, sine = rotations(diagonal(uu), diagonal(ul), diagonal(ll), round_index)
        cosine_col, sine_col = stood(cosine), stood(sine)
        a, b = shift(*turn(uu[...], ul[...], cosine, sine), 1)
        c, d = shift(*turn(lu[...], ll[...], cosine, sine), 1)
        uu[...], lu[...] = shift(*turn(a, c, cosine_col, sine_col), 0)
        ul[...], ll[...] = shift(*turn(b, d, cosine_col, sine_col), 0)
        qu[...], ql[...] = shift(*turn(qu[...], ql[...], cosine, sine), 1)
    end = placing(offset + ROUNDS)
    rotation = dot(jnp.concatenate([qu[...], ql[...]], axis=1), end, (1, 1))
    upper = jnp.concatenate([uu[...], ul[...]], axis=1)
    lower = jnp.concatenate([lu[...], ll[...]], axis=1)
    rotated_gram = dot(end, dot(jnp.concatenate([upper, lower], axis=0), end, (1, 1)))
    return rotation, rotated_gram


def jacobi_kernel(offset, gram, rotation, rotated_gram, *parts):
    rotation[...], rotated_gram[...] = jacobi(gram[...], offset, parts)


def jacobi_rounds(gram, offset):
    square = jax.ShapeDtypeStruct((N, N), jnp.float32)
    return pl.pallas_call(
        functools.partial(jacobi_kernel, offset),
        out_shape=[square, square],
        scratch_shapes=[pltpu.VMEM((HALF, HALF), jnp.float32)] * 4 + [pltpu.VMEM((N, HALF), jnp.float32)] * 2,
        compiler_params=pltpu.CompilerParams(vmem_limit_bytes=16 * 2**20),
    )(gram)


def summed(partial, axis):
    count = lax.axis_size(axis)
    rows, columns = partial.shape
    pieces = partial.reshape(count, rows // count, columns)
    own = jnp.sum(lax.all_to_all(pieces, axis, 0, 0, tiled=True), axis=0)
    spread = jnp.broadcast_to(own[None], pieces.shape)
    return lax.all_to_all(spread, axis, 0, 0, tiled=True).reshape(rows, columns)


def shards(matrix, sender_slot):
    devices = lax.axis_size("blk")
    route = [((i - 1) % devices, i) for i in range(devices)]
    pair_cols = matrix
    gram = summed(dot(matrix, matrix, (0, 0)), "row")
    for step in range(STEPS):
        rotation, rotated_gram = jacobi_rounds(gram, step * ROUNDS)
        second = sender_slot[step, 0] == 1

        def halves(values):
            first_half, second_half = values[:, :HALF], values[:, HALF:]
            return jnp.where(second, first_half, second_half), jnp.where(second, second_half, first_half)

        keep, move = halves(rotation)
        arrived = lax.ppermute(dot(pair_cols, move), "blk", route)
        kept = dot(pair_cols, keep)
        pair_cols = jnp.concatenate([kept, arrived], axis=1)
        if step + 1 < STEPS:
            keep_rows, move_rows = halves(rotated_gram.T)
            moved_gram = lax.ppermute(halves(move_rows.T)[1], "blk", route)
            kept_gram = halves(keep_rows.T)[0]
            cross = summed(dot(kept, arrived, (0, 0)), "row")
            upper = jnp.concatenate([kept_gram, cross], axis=1)
            lower = jnp.concatenate([cross.T, moved_gram], axis=1)
            gram = jnp.concatenate([upper, lower], axis=0)
    return pair_cols


def solution(mesh):
    return jax.shard_map(
        shards,
        mesh=mesh,
        in_specs=(P("row", "blk"), P(None, "blk")),
        out_specs=P("row", "blk"),
        check_vma=False,
    )
```

```python
import jax
import jax.numpy as jnp
from jax import lax
from jax.experimental import pallas as pl
from jax.experimental.pallas import tpu as pltpu
from jax.sharding import PartitionSpec as P

STEPS = 4
ROUNDS = 8
N = 256
HALF = 128
PERIOD = N - 1


def dot(left, right, over=(1, 0)):
    return lax.dot_general(
        left,
        right,
        (((over[0],), (over[1],)), ((), ())),
        precision=lax.Precision.HIGHEST,
        preferred_element_type=jnp.float32,
    )


def seats(position, round_index):
    upper = position + round_index
    upper = jnp.where(upper >= PERIOD, upper - PERIOD, upper)
    lower = round_index - (position - HALF)
    lower = jnp.where(lower < 0, lower + PERIOD, lower)
    return jnp.where(position < HALF, upper, jnp.where(position == HALF, PERIOD, lower))


def placing(round_index, swapped=None):
    index = lax.broadcasted_iota(jnp.int32, (N, N), 0)
    if swapped is not None:
        index = jnp.where(swapped, jnp.where(index < HALF, index + HALF, index - HALF), index)
    position = lax.broadcasted_iota(jnp.int32, (N, N), 1)
    return (index == seats(position, round_index)).astype(jnp.float32)


def rotations(upper_diag, coupling, lower_diag, round_index):
    position = lax.broadcasted_iota(jnp.int32, (1, HALF), 1)
    is_lower = seats(position, round_index) < seats(position + HALF, round_index)
    difference = jnp.where(is_lower, lower_diag - upper_diag, upper_diag - lower_diag)
    x = jnp.abs(difference)
    y = jnp.where(difference >= 0.0, 2.0 * coupling, -2.0 * coupling)
    largest = jnp.maximum(x, jnp.abs(y))
    scale = jnp.where(largest > 0.0, largest, 1.0)
    x = jnp.where(largest > 0.0, x / scale, 1.0)
    y = y / scale
    tangent = y / (x + jnp.sqrt(x * x + y * y))
    cosine = 1.0 / jnp.sqrt(1.0 + tangent * tangent)
    sine = tangent * cosine
    return cosine, jnp.where(is_lower, -sine, sine)


def turn(upper, lower, cosine, sine):
    return cosine * upper + sine * lower, cosine * lower - sine * upper


def shift(upper, lower, axis):
    at = lax.broadcasted_iota(jnp.int32, upper.shape, axis)
    new_upper = jnp.where(at == HALF - 1, lower, pltpu.roll(upper, HALF - 1, axis))
    moved = pltpu.roll(jnp.where(at == 0, upper, lower), 1, axis)
    return new_upper, jnp.where(at == 0, lower, moved)


def jacobi(gram, offset, second, parts):
    uu, ul, lu, ll, qu, ql = parts
    start = placing(offset)
    laid_out = dot(start, dot(gram, start), (0, 0))
    uu[...] = laid_out[:HALF, :HALF]
    ul[...] = laid_out[:HALF, HALF:]
    lu[...] = laid_out[HALF:, :HALF]
    ll[...] = laid_out[HALF:, HALF:]
    qu[...] = start[:, :HALF]
    ql[...] = start[:, HALF:]
    shape = (HALF, HALF)
    eye = lax.broadcasted_iota(jnp.int32, shape, 0) == lax.broadcasted_iota(jnp.int32, shape, 1)

    def diagonal(ref):
        return jnp.sum(jnp.where(eye, ref[...], 0.0), axis=0, keepdims=True)

    def stood(row):
        return jnp.sum(jnp.where(eye, jnp.broadcast_to(row, shape), 0.0), axis=1, keepdims=True)

    for round_index in range(offset, offset + ROUNDS):
        cosine, sine = rotations(diagonal(uu), diagonal(ul), diagonal(ll), round_index)
        cosine_col, sine_col = stood(cosine), stood(sine)
        a, b = shift(*turn(uu[...], ul[...], cosine, sine), 1)
        c, d = shift(*turn(lu[...], ll[...], cosine, sine), 1)
        uu[...], lu[...] = shift(*turn(a, c, cosine_col, sine_col), 0)
        ul[...], ll[...] = shift(*turn(b, d, cosine_col, sine_col), 0)
        qu[...], ql[...] = shift(*turn(qu[...], ql[...], cosine, sine), 1)
    end = placing(offset + ROUNDS, second == 0)
    rotation = dot(jnp.concatenate([qu[...], ql[...]], axis=1), end, (1, 1))
    upper = jnp.concatenate([uu[...], ul[...]], axis=1)
    lower = jnp.concatenate([lu[...], ll[...]], axis=1)
    rotated_gram = dot(end, dot(jnp.concatenate([upper, lower], axis=0), end, (1, 1)))
    return rotation, rotated_gram


def joined(kept_gram, cross, moved_gram):
    upper = jnp.concatenate([kept_gram, cross], axis=1)
    lower = jnp.concatenate([cross.T, moved_gram], axis=1)
    return jnp.concatenate([upper, lower], axis=0)


def step0_kernel(second, gram, out, h0, *parts):
    q0, h0[...] = jacobi(gram[...], 0, second[0, 0], parts)
    out[:N] = q0
    out[N:] = h0[HALF:]


def step1_kernel(second, c1, out0, h0, in0, out, h1, r1, *parts):
    q0, q0_p = out0[:N], in0[:N]
    r1[...] = dot(dot(q0, c1[...], (0, 0)), q0_p)
    gram = joined(h0[:HALF, :HALF], r1[:HALF, HALF:], in0[N:, HALF:])
    q1, h1[...] = jacobi(gram, ROUNDS, second[1, 0], parts)
    out[:N] = q1
    out[N : N + HALF] = h1[HALF:]
    out[N + HALF : 2 * N] = r1[HALF:]
    out[2 * N :] = q0_p


def cross2_kernel(c2, out0, in0, out1, in1, h1, r1, out, kept, gram):
    q0, q0_pp = out0[:N], in1[2 * N :]
    r2 = dot(dot(q0, c2[...], (0, 0)), q0_pp)
    q1, q1_p = out1[:N], in1[:N]
    upper = jnp.concatenate([r1[:HALF, :HALF], r2[:HALF, HALF:]], axis=1)
    lower = jnp.concatenate([in0[N:, :HALF], in1[N + HALF : 2 * N, HALF:]], axis=1)
    s1 = dot(dot(q1, jnp.concatenate([upper, lower], axis=0), (0, 0)), q1_p)
    gram[...] = joined(h1[:HALF, :HALF], s1[:HALF, HALF:], in1[N : N + HALF, HALF:])
    out[:HALF] = s1[HALF:, HALF:]
    out[HALF:N] = r2[HALF:, HALF:]
    out[N : 2 * N] = q1_p[:, HALF:]
    out[2 * N :] = q0_pp[:, HALF:]
    kept[:HALF] = s1[:HALF, :HALF]
    kept[HALF:] = r2[:HALF, :HALF]


def step2_kernel(second, gram, out, q2, h2, *parts):
    q2[...], h2[...] = jacobi(gram[...], 2 * ROUNDS, second[2, 0], parts)
    out[:N] = q2[:, HALF:]
    out[N:] = h2[HALF:, HALF:]


def cross3_kernel(out0, out1, in1, kept, q2, in2a, in2b, cross, left, right):
    q0_k, q1_k, q2_k = out0[:N, :HALF], out1[:N, :HALF], q2[:, :HALF]
    q2_p, q1_pp, q0_ppp = in2b[:N], in2a[N : 2 * N], in2a[2 * N :]
    upper = jnp.concatenate([kept[HALF:], jnp.zeros((HALF, HALF), jnp.float32)], axis=1)
    lower = jnp.concatenate([in1[N + HALF : 2 * N, :HALF], in2a[HALF:N]], axis=1)
    t = dot(dot(q1_k, jnp.concatenate([upper, lower], axis=0), (0, 0)), q1_pp)
    upper = jnp.concatenate([kept[:HALF], t], axis=1)
    lower = jnp.concatenate([in1[N : N + HALF, :HALF], in2a[:HALF]], axis=1)
    cross[...] = dot(dot(q2_k, jnp.concatenate([upper, lower], axis=0), (0, 0)), q2_p)
    left[...] = dot(q0_k, dot(q1_k[:HALF], q2_k[:HALF]))
    right[...] = dot(q0_ppp, dot(q1_pp[HALF:], q2_p[HALF:]))


def step3_kernel(second, c3, cross, left, right, h2, in2b, q3, *parts):
    total = cross[...] + dot(left[...], dot(c3[...], right[...]), (0, 0))
    gram = joined(h2[:HALF, :HALF], total, in2b[N:])
    q3[...], _ = jacobi(gram, 3 * ROUNDS, second[3, 0], parts)


JACOBI_PARTS = [pltpu.VMEM((HALF, HALF), jnp.float32)] * 4 + [pltpu.VMEM((N, HALF), jnp.float32)] * 2


def run(kernel, shapes, *operands, solves=True):
    vmem, smem = pl.BlockSpec(memory_space=pltpu.VMEM), pl.BlockSpec(memory_space=pltpu.SMEM)
    return pl.pallas_call(
        kernel,
        out_shape=[jax.ShapeDtypeStruct(shape, jnp.float32) for shape in shapes],
        in_specs=[smem if x.dtype == jnp.int32 else vmem for x in operands],
        out_specs=[vmem] * len(shapes),
        scratch_shapes=JACOBI_PARTS if solves else [],
        compiler_params=pltpu.CompilerParams(vmem_limit_bytes=16 * 2**20),
        cost_estimate=pl.CostEstimate(flops=10**6, bytes_accessed=2**10, transcendentals=0),
    )(*operands)


def shards(matrix, sender_slot):
    devices, count = lax.axis_size("blk"), lax.axis_size("row")
    route = [((i - 1) % devices, i) for i in range(devices)]

    def onward(values):
        return lax.ppermute(values, "blk", route)

    def exchange(pieces):
        return lax.all_to_all(pieces, "row", 0, 0, tiled=True)

    def pieces_of(partial):
        return partial.reshape(count, N // count, N)

    def spread(received):
        own = jnp.sum(received, axis=0, keepdims=True)
        return jnp.broadcast_to(own, (count, N // count, N))

    height = N // count
    before1 = onward(matrix)
    before2 = onward(before1)
    before3 = onward(before2)
    received = exchange(pieces_of(dot(matrix, matrix, (0, 0))))
    gathered = []
    for other in (before1, before2, before3):
        parts = pieces_of(dot(matrix, other, (0, 0)))
        both = exchange(jnp.concatenate([spread(received), parts], axis=1))
        gathered.append(both[:, :height].reshape(N, N))
        received = both[:, height:]
    gathered.append(exchange(spread(received)).reshape(N, N))
    c0, c1, c2, c3 = gathered

    def rotated(pair_cols, rotation):
        arrived = onward(dot(pair_cols, rotation[:, HALF:]))
        return jnp.concatenate([dot(pair_cols, rotation[:, :HALF]), arrived], axis=1)

    square, block = (N, N), (HALF, HALF)
    out0, h0 = run(step0_kernel, [(N + HALF, N), square], sender_slot, c0)
    in0 = onward(out0)
    pair_cols = rotated(matrix, out0[:N])
    out1, h1, r1 = run(step1_kernel, [(3 * N, N), square, square], sender_slot, c1, out0, h0, in0)
    in1 = onward(out1)
    pair_cols = rotated(pair_cols, out1[:N])
    out2a, kept, gram2 = run(
        cross2_kernel, [(3 * N, HALF), (N, HALF), square], c2, out0, in0, out1, in1, h1, r1, solves=False
    )
    in2a = onward(out2a)
    out2b, q2, h2 = run(step2_kernel, [(N + HALF, HALF), square, square], sender_slot, gram2)
    in2b = onward(out2b)
    pair_cols = rotated(pair_cols, q2)
    cross, left, right = run(
        cross3_kernel, [block, (N, HALF), (N, HALF)], out0, out1, in1, kept, q2, in2a, in2b, solves=False
    )
    (q3,) = run(step3_kernel, [square], sender_slot, c3, cross, left, right, h2, in2b)
    return rotated(pair_cols, q3)


def solution(mesh):
    return jax.shard_map(
        shards,
        mesh=mesh,
        in_specs=(P("row", "blk"), P(None, "blk")),
        out_specs=P("row", "blk"),
        check_vma=False,
    )
```

```python
import jax
import jax.numpy as jnp
from jax import lax
from jax.experimental import pallas as pl
from jax.experimental.pallas import tpu as pltpu
from jax.sharding import PartitionSpec as P

STEPS = 4
ROUNDS = 8
N = 256
HALF = 128
TILES = 64
PERIOD = N - 1


def dot(left, right, over=(1, 0), precision=lax.Precision.HIGHEST):
    return lax.dot_general(
        left,
        right,
        (((over[0],), (over[1],)), ((), ())),
        precision=precision,
        preferred_element_type=jnp.float32,
    )


def seats(position, round_index):
    upper = position + round_index
    upper = jnp.where(upper >= PERIOD, upper - PERIOD, upper)
    lower = round_index - (position - HALF)
    lower = jnp.where(lower < 0, lower + PERIOD, lower)
    return jnp.where(position < HALF, upper, jnp.where(position == HALF, PERIOD, lower))


def placing(round_index, swapped=None):
    index = lax.broadcasted_iota(jnp.int32, (N, N), 0)
    if swapped is not None:
        index = jnp.where(swapped, jnp.where(index < HALF, index + HALF, index - HALF), index)
    position = lax.broadcasted_iota(jnp.int32, (N, N), 1)
    return (index == seats(position, round_index)).astype(jnp.bfloat16)


def thirds(values):
    high = values.astype(jnp.bfloat16)
    rest = values - high.astype(jnp.float32)
    middle = rest.astype(jnp.bfloat16)
    return high, middle, (rest - middle.astype(jnp.float32)).astype(jnp.bfloat16)


def placed(pieces, place, over):
    numbers = (((1,), (over,)), ((), ()))
    return [lax.dot_general(x, place, numbers, preferred_element_type=jnp.float32) for x in pieces]


def laid_both(values, place, over):
    columns = [x.astype(jnp.bfloat16) for x in placed(thirds(values), place, over)]
    numbers = (((over,), (0,)), ((), ()))
    return sum(lax.dot_general(place, x, numbers, preferred_element_type=jnp.float32) for x in columns)


def rotations(upper_diag, coupling, lower_diag, round_index):
    position = lax.broadcasted_iota(jnp.int32, (1, HALF), 1)
    is_lower = seats(position, round_index) < seats(position + HALF, round_index)
    difference = jnp.where(is_lower, lower_diag - upper_diag, upper_diag - lower_diag)
    x = jnp.abs(difference)
    y = jnp.where(difference >= 0.0, 2.0 * coupling, -2.0 * coupling)
    largest = jnp.maximum(x, jnp.abs(y))
    scale = jnp.where(largest > 0.0, largest, 1.0)
    x = jnp.where(largest > 0.0, x / scale, 1.0)
    y = y / scale
    tangent = y / (x + jnp.sqrt(x * x + y * y))
    cosine = 1.0 / jnp.sqrt(1.0 + tangent * tangent)
    sine = tangent * cosine
    return cosine, jnp.where(is_lower, -sine, sine)


def turn(upper, lower, cosine, sine):
    return cosine * upper + sine * lower, cosine * lower - sine * upper


def shift(upper, lower, axis):
    at = lax.broadcasted_iota(jnp.int32, upper.shape, axis)
    new_upper = jnp.where(at == HALF - 1, lower, pltpu.roll(upper, HALF - 1, axis))
    moved = pltpu.roll(jnp.where(at == 0, upper, lower), 1, axis)
    return new_upper, jnp.where(at == 0, lower, moved)


def jacobi(gram, offset, second, parts):
    uu, ul, lu, ll, qu, ql = parts
    start = placing(offset)
    laid_out = laid_both(gram, start, 0)
    uu[...] = laid_out[:HALF, :HALF]
    ul[...] = laid_out[:HALF, HALF:]
    lu[...] = laid_out[HALF:, :HALF]
    ll[...] = laid_out[HALF:, HALF:]
    qu[...] = start[:, :HALF].astype(jnp.float32)
    ql[...] = start[:, HALF:].astype(jnp.float32)
    shape = (HALF, HALF)
    eye = lax.broadcasted_iota(jnp.int32, shape, 0) == lax.broadcasted_iota(jnp.int32, shape, 1)

    def diagonal(ref):
        return jnp.sum(jnp.where(eye, ref[...], 0.0), axis=0, keepdims=True)

    def stood(row):
        return jnp.sum(jnp.where(eye, jnp.broadcast_to(row, shape), 0.0), axis=1, keepdims=True)

    for round_index in range(offset, offset + ROUNDS):
        cosine, sine = rotations(diagonal(uu), diagonal(ul), diagonal(ll), round_index)
        cosine_col, sine_col = stood(cosine), stood(sine)
        a, b = shift(*turn(uu[...], ul[...], cosine, sine), 1)
        c, d = shift(*turn(lu[...], ll[...], cosine, sine), 1)
        uu[...], lu[...] = shift(*turn(a, c, cosine_col, sine_col), 0)
        ul[...], ll[...] = shift(*turn(b, d, cosine_col, sine_col), 0)
        qu[...], ql[...] = shift(*turn(qu[...], ql[...], cosine, sine), 1)
    end = placing(offset + ROUNDS, second == 0)
    rotation = sum(placed(thirds(jnp.concatenate([qu[...], ql[...]], axis=1)), end, 1))
    upper = jnp.concatenate([uu[...], ul[...]], axis=1)
    lower = jnp.concatenate([lu[...], ll[...]], axis=1)
    rotated_gram = laid_both(jnp.concatenate([upper, lower], axis=0), end, 1)
    return rotation, rotated_gram


def joined(kept_gram, cross, moved_gram):
    upper = jnp.concatenate([kept_gram, cross], axis=1)
    lower = jnp.concatenate([cross.T, moved_gram], axis=1)
    return jnp.concatenate([upper, lower], axis=0)


def tiles(square):
    sides = [square[:, :HALF].reshape(-1, 1, 8, HALF), square[:, HALF:].reshape(-1, 1, 8, HALF)]
    return jnp.concatenate(sides, axis=1)


def square_of(received, place):
    count, height = received.shape[0], TILES // received.shape[0] * 8
    part = received[:, place * height : (place + 1) * height, :].reshape(TILES // 2, 2, 8, HALF)
    return jnp.concatenate([part[:, 0].reshape(N, HALF), part[:, 1].reshape(N, HALF)], axis=1)


def pack_kernel(skipped, received, *refs):
    *blocks, out = refs
    count, height = out.shape[0], TILES // out.shape[0] * 8
    if received is not None:
        spread = received.shape[1] - skipped * height
        own = jnp.sum(received[:, skipped * height :, :], axis=0, keepdims=True)
        out[:, :spread, :] = jnp.broadcast_to(own, (count, spread, HALF))
    else:
        spread = 0
    for number, block in enumerate(blocks):
        at = spread + number * height
        out[:, at : at + height, :] = tiles(block[...]).reshape(count, height, HALF)


def step0_kernel(second, received, out, h0, *parts):
    q0, h0[...] = jacobi(square_of(received, 0), 0, second[0, 0], parts)
    out[:N] = q0
    out[N:] = h0[HALF:]


def step1_kernel(second, received, out0, h0, in0, out, h1, r1, *parts):
    q0, q0_p = out0[:N], in0[:N]
    r1[...] = dot(dot(q0, square_of(received, 0), (0, 0)), q0_p)
    gram = joined(h0[:HALF, :HALF], r1[:HALF, HALF:], in0[N:, HALF:])
    q1, h1[...] = jacobi(gram, ROUNDS, second[1, 0], parts)
    out[:N] = q1
    out[N : N + HALF] = h1[HALF:]
    out[N + HALF : 2 * N] = r1[HALF:]
    out[2 * N :] = q0_p


def cross2_kernel(received, out0, in0, out1, in1, h1, r1, out, kept, gram):
    q0, q0_pp = out0[:N], in1[2 * N :]
    r2 = dot(dot(q0, square_of(received, 1), (0, 0)), q0_pp)
    q1, q1_p = out1[:N], in1[:N]
    upper = jnp.concatenate([r1[:HALF, :HALF], r2[:HALF, HALF:]], axis=1)
    lower = jnp.concatenate([in0[N:, :HALF], in1[N + HALF : 2 * N, HALF:]], axis=1)
    s1 = dot(dot(q1, jnp.concatenate([upper, lower], axis=0), (0, 0)), q1_p)
    gram[...] = joined(h1[:HALF, :HALF], s1[:HALF, HALF:], in1[N : N + HALF, HALF:])
    out[:HALF] = s1[HALF:, HALF:]
    out[HALF:N] = r2[HALF:, HALF:]
    out[N : 2 * N] = q1_p[:, HALF:]
    out[2 * N :] = q0_pp[:, HALF:]
    kept[:HALF] = s1[:HALF, :HALF]
    kept[HALF:] = r2[:HALF, :HALF]


def step2_kernel(second, gram, out, q2, h2, *parts):
    q2[...], h2[...] = jacobi(gram[...], 2 * ROUNDS, second[2, 0], parts)
    out[:N] = q2[:, HALF:]
    out[N:] = h2[HALF:, HALF:]


def cross3_kernel(out0, out1, in1, kept, q2, in2a, in2b, cross, left, right):
    q0_k, q1_k, q2_k = out0[:N, :HALF], out1[:N, :HALF], q2[:, :HALF]
    q2_p, q1_pp, q0_ppp = in2b[:N], in2a[N : 2 * N], in2a[2 * N :]
    upper = jnp.concatenate([kept[HALF:], jnp.zeros((HALF, HALF), jnp.float32)], axis=1)
    lower = jnp.concatenate([in1[N + HALF : 2 * N, :HALF], in2a[HALF:N]], axis=1)
    t = dot(dot(q1_k, jnp.concatenate([upper, lower], axis=0), (0, 0)), q1_pp)
    upper = jnp.concatenate([kept[:HALF], t], axis=1)
    lower = jnp.concatenate([in1[N : N + HALF, :HALF], in2a[:HALF]], axis=1)
    cross[...] = dot(dot(q2_k, jnp.concatenate([upper, lower], axis=0), (0, 0)), q2_p)
    left[...] = dot(q0_k, dot(q1_k[:HALF], q2_k[:HALF]))
    right[...] = dot(q0_ppp, dot(q1_pp[HALF:], q2_p[HALF:]))


def weights_kernel(in0, in1, in2a, in2b, out):
    q2_k, q2_m = in2b[:HALF], in2b[HALF:N]
    q1_pp, q0_pp = in2a[N : 2 * N], in1[2 * N :]
    out[:N] = dot(in0[:N, :HALF], dot(in1[:HALF, :HALF], q2_k))
    travelled = dot(q0_pp[:, HALF:], dot(in1[HALF:N, :HALF], q2_k))
    out[N : 2 * N] = travelled + dot(q0_pp[:, :HALF], dot(q1_pp[:HALF], q2_m))
    out[2 * N :] = dot(in2a[2 * N :], dot(q1_pp[HALF:], q2_m))


def step3_kernel(second, received, cross, left, right, h2, in2b, q3, *parts):
    total = cross[...] + dot(left[...], dot(square_of(received, 0), right[...]), (0, 0))
    gram = joined(h2[:HALF, :HALF], total, in2b[N:])
    q3[...], _ = jacobi(gram, 3 * ROUNDS, second[3, 0], parts)


JACOBI_PARTS = [pltpu.VMEM((HALF, HALF), jnp.float32)] * 4 + [pltpu.VMEM((N, HALF), jnp.float32)] * 2


def run(kernel, shapes, *operands, solves=True, last=()):
    vmem, smem = pl.BlockSpec(memory_space=pltpu.VMEM), pl.BlockSpec(memory_space=pltpu.SMEM)
    specs = [smem if x.dtype == jnp.int32 else vmem for x in operands] + [pl.BlockSpec(memory_space=pl.ANY)] * len(last)

    def body(*refs):
        given = len(operands)
        kernel(*refs[:given], *refs[given + len(last) :])

    return pl.pallas_call(
        body,
        out_shape=[jax.ShapeDtypeStruct(shape, jnp.float32) for shape in shapes],
        in_specs=specs,
        out_specs=[vmem] * len(shapes),
        scratch_shapes=JACOBI_PARTS if solves else [],
        compiler_params=pltpu.CompilerParams(vmem_limit_bytes=16 * 2**20),
        cost_estimate=pl.CostEstimate(flops=10**6, bytes_accessed=2**10, transcendentals=0),
    )(*operands, *last)


def product(left, right, over=(1, 0)):
    return dot(left, right, over, lax.Precision.HIGH)


def shards(matrix, sender_slot):
    devices, count = lax.axis_size("blk"), lax.axis_size("row")

    def onward(values, places=1):
        return lax.ppermute(values, "blk", [((i - places) % devices, i) for i in range(devices)])

    def exchange(received, skipped, *blocks, last=()):
        height = TILES // count * 8
        given = [] if received is None else [received]
        total = len(blocks) * height + (0 if received is None else received.shape[1] - skipped * height)

        def kernel(*refs):
            pack_kernel(skipped, refs[0] if given else None, *refs[len(given) :])

        (pieces,) = run(kernel, [(count, total, HALF)], *given, *blocks, solves=False, last=last)
        return lax.all_to_all(pieces, "row", 0, 0, tiled=True)

    def rotated(pair_cols, rotation):
        arrived = onward(product(pair_cols, rotation[:, HALF:]))
        return jnp.concatenate([product(pair_cols, rotation[:, :HALF]), arrived], axis=1)

    square, block = (N, N), (HALF, HALF)
    before1, before2 = onward(matrix), onward(matrix, 2)
    received = exchange(None, 0, product(matrix, matrix, (0, 0)))
    c1, c2 = product(matrix, before1, (0, 0)), product(matrix, before2, (0, 0))
    with_gram = exchange(received, 0, c1, c2)
    before3 = onward(before2)
    c3 = product(matrix, before3, (0, 0))
    with_c12 = exchange(with_gram, 1, c3)
    out0, h0 = run(step0_kernel, [(N + HALF, N), square], sender_slot, with_gram)
    in0 = onward(out0)
    pair_cols = rotated(matrix, out0[:N])
    out1, h1, r1 = run(step1_kernel, [(3 * N, N), square, square], sender_slot, with_c12, out0, h0, in0)
    in1 = onward(out1)
    with_c3 = exchange(with_c12, 2, last=(out1,))
    pair_cols = rotated(pair_cols, out1[:N])
    out2a, kept, gram2 = run(
        cross2_kernel, [(3 * N, HALF), (N, HALF), square], with_c12, out0, in0, out1, in1, h1, r1, solves=False
    )
    in2a = onward(out2a)
    out2b, q2, h2 = run(step2_kernel, [(N + HALF, HALF), square, square], sender_slot, gram2)
    in2b = onward(out2b)
    cross, left, right = run(
        cross3_kernel, [block, (N, HALF), (N, HALF)], out0, out1, in1, kept, q2, in2a, in2b, solves=False
    )
    (weights,) = run(weights_kernel, [(3 * N, HALF)], in0, in1, in2a, in2b, solves=False)
    arrived = (
        product(before1, weights[:N]) + product(before2, weights[N : 2 * N]) + product(before3, weights[2 * N :])
    )
    pair_cols = jnp.concatenate([product(pair_cols, q2[:, :HALF]), arrived], axis=1)
    (q3,) = run(step3_kernel, [square], sender_slot, with_c3, cross, left, right, h2, in2b)
    return rotated(pair_cols, q3)


def solution(mesh):
    return jax.shard_map(
        shards,
        mesh=mesh,
        in_specs=(P("row", "blk"), P(None, "blk")),
        out_specs=P("row", "blk"),
        check_vma=False,
    )
```

```python
import functools

import jax
import jax.numpy as jnp
from jax import lax
from jax.experimental import pallas as pl
from jax.experimental.pallas import tpu as pltpu
from jax.sharding import PartitionSpec as P

STEPS = 4
ROUNDS = 8
N = 256
HALF = 128
TILES = 64
PERIOD = N - 1


def dot(left, right, over=(1, 0), precision=lax.Precision.HIGHEST):
    return lax.dot_general(
        left,
        right,
        (((over[0],), (over[1],)), ((), ())),
        precision=precision,
        preferred_element_type=jnp.float32,
    )


def halved(values):
    high = values.astype(jnp.bfloat16)
    return high, (values - high.astype(jnp.float32)).astype(jnp.bfloat16)


def cross_dot(left, right, over=(1, 0)):
    numbers = (((over[0],), (over[1],)), ((), ()))
    (a, b), (c, d) = halved(left), halved(right)
    passes = [lax.dot_general(x, y, numbers, preferred_element_type=jnp.float32) for x, y in ((a, d), (b, c), (a, c))]
    return passes[0] + passes[1] + passes[2]


def seats(position, round_index):
    upper = position + round_index
    upper = jnp.where(upper >= PERIOD, upper - PERIOD, upper)
    lower = round_index - (position - HALF)
    lower = jnp.where(lower < 0, lower + PERIOD, lower)
    return jnp.where(position < HALF, upper, jnp.where(position == HALF, PERIOD, lower))


def placing(round_index, swapped=None):
    index = lax.broadcasted_iota(jnp.int32, (N, N), 0)
    if swapped is not None:
        index = jnp.where(swapped, jnp.where(index < HALF, index + HALF, index - HALF), index)
    position = lax.broadcasted_iota(jnp.int32, (N, N), 1)
    return (index == seats(position, round_index)).astype(jnp.bfloat16)


def thirds(values):
    high = values.astype(jnp.bfloat16)
    rest = values - high.astype(jnp.float32)
    middle = rest.astype(jnp.bfloat16)
    return high, middle, (rest - middle.astype(jnp.float32)).astype(jnp.bfloat16)


def placed(pieces, place, over):
    numbers = (((1,), (over,)), ((), ()))
    return [lax.dot_general(x, place, numbers, preferred_element_type=jnp.float32) for x in pieces]


def laid_both(values, place, over):
    columns = [x.astype(jnp.bfloat16) for x in placed(thirds(values), place, over)]
    numbers = (((over,), (0,)), ((), ()))
    return sum(lax.dot_general(place, x, numbers, preferred_element_type=jnp.float32) for x in columns)


def rotations(upper_diag, coupling, lower_diag, round_index):
    position = lax.broadcasted_iota(jnp.int32, (1, HALF), 1)
    is_lower = seats(position, round_index) < seats(position + HALF, round_index)
    difference = jnp.where(is_lower, lower_diag - upper_diag, upper_diag - lower_diag)
    x = jnp.abs(difference)
    y = jnp.where(difference >= 0.0, 2.0 * coupling, -2.0 * coupling)
    largest = jnp.maximum(x, jnp.abs(y))
    scale = jnp.where(largest > 0.0, largest, 1.0)
    inverse = 1.0 / scale
    x = jnp.where(largest > 0.0, x * inverse, 1.0)
    y = y * inverse
    tangent = y / (x + jnp.sqrt(x * x + y * y))
    cosine = 1.0 / jnp.sqrt(1.0 + tangent * tangent)
    sine = tangent * cosine
    return cosine, jnp.where(is_lower, -sine, sine)


def turn(upper, lower, cosine, sine):
    return cosine * upper + sine * lower, cosine * lower - sine * upper


def shift(upper, lower, axis):
    at = lax.broadcasted_iota(jnp.int32, upper.shape, axis)
    new_upper = jnp.where(at == HALF - 1, lower, pltpu.roll(upper, HALF - 1, axis))
    moved = pltpu.roll(jnp.where(at == 0, upper, lower), 1, axis)
    return new_upper, jnp.where(at == 0, lower, moved)


def jacobi(gram, offset, second, parts):
    uu, ul, lu, ll, qu, ql = parts
    start = placing(offset)
    laid_out = laid_both(gram, start, 0)
    uu[...] = laid_out[:HALF, :HALF]
    ul[...] = laid_out[:HALF, HALF:]
    lu[...] = laid_out[HALF:, :HALF]
    ll[...] = laid_out[HALF:, HALF:]
    qu[...] = start[:, :HALF].astype(jnp.float32)
    ql[...] = start[:, HALF:].astype(jnp.float32)
    shape = (HALF, HALF)
    eye = lax.broadcasted_iota(jnp.int32, shape, 0) == lax.broadcasted_iota(jnp.int32, shape, 1)

    def diagonal(ref):
        return jnp.sum(jnp.where(eye, ref[...], 0.0), axis=0, keepdims=True)

    def stood(row):
        return jnp.sum(jnp.where(eye, jnp.broadcast_to(row, shape), 0.0), axis=1, keepdims=True)

    for round_index in range(offset, offset + ROUNDS):
        cosine, sine = rotations(diagonal(uu), diagonal(ul), diagonal(ll), round_index)
        cosine_col, sine_col = stood(cosine), stood(sine)
        a, b = shift(*turn(uu[...], ul[...], cosine, sine), 1)
        c, d = shift(*turn(lu[...], ll[...], cosine, sine), 1)
        uu[...], lu[...] = shift(*turn(a, c, cosine_col, sine_col), 0)
        ul[...], ll[...] = shift(*turn(b, d, cosine_col, sine_col), 0)
        qu[...], ql[...] = shift(*turn(qu[...], ql[...], cosine, sine), 1)
    end = placing(offset + ROUNDS, second == 0)
    rotation = sum(placed(thirds(jnp.concatenate([qu[...], ql[...]], axis=1)), end, 1))
    upper = jnp.concatenate([uu[...], ul[...]], axis=1)
    lower = jnp.concatenate([lu[...], ll[...]], axis=1)
    rotated_gram = laid_both(jnp.concatenate([upper, lower], axis=0), end, 1)
    return rotation, rotated_gram


def joined(kept_gram, cross, moved_gram):
    upper = jnp.concatenate([kept_gram, cross], axis=1)
    lower = jnp.concatenate([cross.T, moved_gram], axis=1)
    return jnp.concatenate([upper, lower], axis=0)


def tiles(square):
    sides = [square[:, :HALF].reshape(-1, 1, 8, HALF), square[:, HALF:].reshape(-1, 1, 8, HALF)]
    return jnp.concatenate(sides, axis=1)


def square_of(received, place):
    count, height = received.shape[0], TILES // received.shape[0] * 8
    part = received[:, place * height : (place + 1) * height, :].reshape(TILES // 2, 2, 8, HALF)
    return jnp.concatenate([part[:, 0].reshape(N, HALF), part[:, 1].reshape(N, HALF)], axis=1)


def pack_kernel(skipped, received, *refs):
    *blocks, out = refs
    count, height = out.shape[0], TILES // out.shape[0] * 8
    if received is not None:
        spread = received.shape[1] - skipped * height
        own = jnp.sum(received[:, skipped * height :, :], axis=0, keepdims=True)
        out[:, :spread, :] = jnp.broadcast_to(own, (count, spread, HALF))
    else:
        spread = 0
    for number, block in enumerate(blocks):
        at = spread + number * height
        out[:, at : at + height, :] = tiles(block[...]).reshape(count, height, HALF)


def step0_kernel(second, received, out, h0, *parts):
    q0, rotated_gram = jacobi(square_of(received, 0), 0, second[0, 0], parts)
    h0[...] = rotated_gram[:HALF, :HALF]
    out[:N] = q0
    out[N:] = rotated_gram[HALF:]


def step1_kernel(second, received, out0, h0, in0, out, carried, *parts):
    r1 = cross_dot(cross_dot(out0[:N], square_of(received, 1), (0, 0)), in0[:N])
    out[N:, HALF:] = r1[HALF:, HALF:]
    carried[:, HALF:] = r1[:, :HALF]
    gram = joined(h0[...], r1[:HALF, HALF:], in0[N:, HALF:])
    q1, h1 = jacobi(gram, ROUNDS, second[1, 0], parts)
    out[:N] = q1
    out[N:, :HALF] = h1[HALF:, HALF:]
    carried[:, :HALF] = h1[:, :HALF]


def cross2_kernel(received, out0, in0, q0_pp, out1, in1, carried, out, kept, gram):
    r2 = cross_dot(cross_dot(out0[:N], square_of(received, 0), (0, 0)), q0_pp[:N])
    upper = jnp.concatenate([carried[:HALF, HALF:], r2[:HALF, HALF:]], axis=1)
    lower = jnp.concatenate([in0[N:, :HALF], in1[N:, HALF:]], axis=1)
    s1 = cross_dot(cross_dot(out1[:N], jnp.concatenate([upper, lower], axis=0), (0, 0)), in1[:N])
    gram[...] = joined(carried[:HALF, :HALF], s1[:HALF, HALF:], in1[N:, :HALF])
    out[:HALF] = s1[HALF:, HALF:]
    out[HALF:N] = r2[HALF:, HALF:]
    out[N : N + HALF] = carried[HALF:, :HALF]
    out[N + HALF : 2 * N] = carried[HALF:, HALF:]
    out[2 * N : 3 * N] = in1[:N, HALF:]
    out[3 * N :] = q0_pp[:N, HALF:]
    kept[:HALF] = s1[:HALF, :HALF]
    kept[HALF:] = r2[:HALF, :HALF]


def step2_kernel(second, gram, out, own, *parts):
    q2, h2 = jacobi(gram[...], 2 * ROUNDS, second[2, 0], parts)
    out[:N] = q2[:, HALF:]
    out[N:] = h2[HALF:, HALF:]
    own[:N] = q2[:, :HALF]
    own[N:] = h2[:HALF, :HALF]


def cross3_kernel(out0, out1, kept, own2, in2a, in2b, cross, left, right):
    q0_k, q1_k, q2_k = out0[:N, :HALF], out1[:N, :HALF], own2[:N]
    q2_p, q1_pp, q0_ppp = in2b[:N], in2a[2 * N : 3 * N], in2a[3 * N :]
    upper = jnp.concatenate([kept[HALF:], jnp.zeros((HALF, HALF), jnp.float32)], axis=1)
    lower = jnp.concatenate([in2a[N + HALF : 2 * N], in2a[HALF:N]], axis=1)
    t = cross_dot(cross_dot(q1_k, jnp.concatenate([upper, lower], axis=0), (0, 0)), q1_pp)
    upper = jnp.concatenate([kept[:HALF], t], axis=1)
    lower = jnp.concatenate([in2a[N : N + HALF], in2a[:HALF]], axis=1)
    cross[...] = cross_dot(cross_dot(q2_k, jnp.concatenate([upper, lower], axis=0), (0, 0)), q2_p)
    left[...] = cross_dot(q0_k, cross_dot(q1_k[:HALF], q2_k[:HALF]))
    right[...] = cross_dot(q0_ppp, cross_dot(q1_pp[HALF:], q2_p[HALF:]))


def weights_kernel(out0, in0, q0_pp, out1, in1, in2a, own2, own, before):
    q2_k, q2_m = own2[:HALF], own2[HALF:N]
    q1_kk, q1_mk, p1_kk, p1_mk = out1[:HALF, :HALF], out1[HALF:N, :HALF], in1[:HALF, :HALF], in1[HALF:N, :HALF]
    p1_km, p1_mm = in1[:HALF, HALF:], in1[HALF:N, HALF:]
    own[:N] = cross_dot(out0[:N, :HALF], cross_dot(q1_kk, q2_k))
    travelled = cross_dot(in0[:N, HALF:], cross_dot(q1_mk, q2_k))
    own[N : 2 * N] = travelled + cross_dot(in0[:N, :HALF], cross_dot(p1_km, q2_m))
    own[2 * N :] = cross_dot(q0_pp[:N, HALF:], cross_dot(p1_mm, q2_m))
    before[:N] = cross_dot(in0[:N, :HALF], p1_kk)
    before[N : 2 * N] = cross_dot(q0_pp[:N, HALF:], p1_mk)
    before[2 * N : 3 * N] = cross_dot(q0_pp[:N, :HALF], in2a[2 * N : 2 * N + HALF])
    before[3 * N :] = cross_dot(in2a[3 * N :], in2a[2 * N + HALF : 3 * N])


def products_kernel(left, right, out):
    step = min(N, left.shape[0])
    out[...] = jnp.zeros(out.shape, jnp.float32)

    def some_rows(number, carry):
        rows = pl.ds(pl.multiple_of(number * step, step), step)
        out[...] += cross_dot(left[rows, :], right[rows, :], (0, 0))
        return carry

    lax.fori_loop(0, left.shape[0] // step, some_rows, 0)


def columns_kernel(x0, x1, x2, x3, own, before, kept, left, right):
    step = min(N, kept.shape[0])

    def some_rows(number, carry):
        rows = pl.ds(pl.multiple_of(number * step, step), step)
        first, second, third, fourth = x0[rows, :], x1[rows, :], x2[rows, :], x3[rows, :]
        kept[rows, :] = cross_dot(first, own[:N]) + cross_dot(second, own[N : 2 * N]) + cross_dot(third, own[2 * N :])
        left[rows, :] = cross_dot(second, before[:N]) + cross_dot(third, before[N : 2 * N])
        right[rows, :] = cross_dot(third, before[2 * N : 3 * N]) + cross_dot(fourth, before[3 * N :])
        return carry

    lax.fori_loop(0, kept.shape[0] // step, some_rows, 0)


def last_kernel(place, pair_cols, rotation, out):
    out[...] = cross_dot(pair_cols[...], rotation[:, place : place + HALF])


def pair_kernel(kept, left, right, in2b, out):
    out[:, :HALF] = kept[...]
    out[:, HALF:] = cross_dot(left[...], in2b[:HALF]) + cross_dot(right[...], in2b[HALF:N])


def step3_kernel(second, received, cross, left, right, own2, in2b, q3, *parts):
    total = cross[...] + cross_dot(left[...], cross_dot(square_of(received, 0), right[...]), (0, 0))
    gram = joined(own2[N:], total, in2b[N:])
    q3[...], _ = jacobi(gram, 3 * ROUNDS, second[3, 0], parts)


JACOBI_PARTS = [pltpu.VMEM((HALF, HALF), jnp.float32)] * 4 + [pltpu.VMEM((N, HALF), jnp.float32)] * 2


def run(kernel, shapes, *operands, solves=True, last=(), vmem=8):
    whole, smem = pl.BlockSpec(memory_space=pltpu.VMEM), pl.BlockSpec(memory_space=pltpu.SMEM)
    specs = [smem if x.dtype == jnp.int32 else whole for x in operands] + [pl.BlockSpec(memory_space=pl.ANY)] * len(last)

    def body(*refs):
        given = len(operands)
        kernel(*refs[:given], *refs[given + len(last) :])

    return pl.pallas_call(
        body,
        out_shape=[jax.ShapeDtypeStruct(shape, jnp.float32) for shape in shapes],
        in_specs=specs,
        out_specs=[whole] * len(shapes),
        scratch_shapes=JACOBI_PARTS if solves else [],
        compiler_params=pltpu.CompilerParams(vmem_limit_bytes=vmem * 2**20),
        cost_estimate=pl.CostEstimate(flops=10**6, bytes_accessed=2**10, transcendentals=0),
    )(*operands, *last)


def shards(matrix, sender_slot):
    devices, count = lax.axis_size("blk"), lax.axis_size("row")

    def onward(values, places=1):
        return lax.ppermute(values, "blk", [((i - places) % devices, i) for i in range(devices)])

    def products(other):
        return run(products_kernel, [(N, N)], matrix, other, solves=False)[0]

    def exchange(received, skipped, *blocks, last=()):
        height = TILES // count * 8
        given = [] if received is None else [received]
        total = len(blocks) * height + (0 if received is None else received.shape[1] - skipped * height)

        def kernel(*refs):
            pack_kernel(skipped, refs[0] if given else None, *refs[len(given) :])

        (pieces,) = run(kernel, [(count, total, HALF)], *given, *blocks, solves=False, last=last)
        return lax.all_to_all(pieces, "row", 0, 0, tiled=True)

    square, block = (N, N), (HALF, HALF)
    before1 = onward(matrix)
    received = exchange(None, 0, products(matrix), products(before1))
    before2 = onward(before1)
    with_c1 = exchange(received, 0, products(before2))
    before3 = onward(before2)
    with_c2 = exchange(with_c1, 2, products(before3))
    out0, h0 = run(step0_kernel, [(N + HALF, N), block], sender_slot, with_c1)
    in0 = onward(out0)
    q0_pp = onward(in0)
    out1, carried = run(step1_kernel, [(N + HALF, N), square], sender_slot, with_c1, out0, h0, in0)
    in1 = onward(out1)
    with_c3 = exchange(with_c2, 1, last=(out1,))
    out2a, kept, gram2 = run(
        cross2_kernel,
        [(4 * N, HALF), (N, HALF), square],
        *(with_c2, out0, in0, q0_pp, out1, in1, carried),
        solves=False,
    )
    in2a = onward(out2a)
    out2b, own2 = run(step2_kernel, [(N + HALF, HALF), (N + HALF, HALF)], sender_slot, gram2)
    in2b = onward(out2b)
    own, before = run(
        weights_kernel, [(3 * N, HALF), (4 * N, HALF)], out0, in0, q0_pp, out1, in1, in2a, own2, solves=False
    )
    kept_cols, left_cols, right_cols = run(
        columns_kernel, [(matrix.shape[0], HALF)] * 3, matrix, before1, before2, before3, own, before, solves=False, vmem=12
    )
    cross, left, right = run(
        cross3_kernel,
        [block, (N, HALF), (N, HALF)],
        *(out0, out1, kept, own2, in2a, in2b),
        solves=False,
        last=(kept_cols,),
    )
    (pair_cols,) = run(pair_kernel, [matrix.shape], kept_cols, left_cols, right_cols, in2b, solves=False)
    (q3,) = run(step3_kernel, [square], sender_slot, with_c3, cross, left, right, own2, in2b, last=(pair_cols,))

    def last_columns(place):
        return run(functools.partial(last_kernel, place), [(matrix.shape[0], HALF)], pair_cols, q3, solves=False)[0]

    arrived = onward(last_columns(HALF))
    kept = last_columns(0)
    return jnp.concatenate([kept, arrived], axis=1)


def solution(mesh):
    return jax.shard_map(
        shards,
        mesh=mesh,
        in_specs=(P("row", "blk"), P(None, "blk")),
        out_specs=P("row", "blk"),
        check_vma=False,
    )
```

```python
import functools

import jax
import jax.numpy as jnp
from jax import lax
from jax.experimental import pallas as pl
from jax.experimental.pallas import tpu as pltpu
from jax.sharding import PartitionSpec as P

STEPS = 4
ROUNDS = 8
N = 256
HALF = 128
TILES = 64
PERIOD = N - 1


def dot(left, right, over=(1, 0), precision=lax.Precision.HIGHEST):
    return lax.dot_general(
        left,
        right,
        (((over[0],), (over[1],)), ((), ())),
        precision=precision,
        preferred_element_type=jnp.float32,
    )


def halved(values):
    high = values.astype(jnp.bfloat16)
    return high, (values - high.astype(jnp.float32)).astype(jnp.bfloat16)


def cross_dot(left, right, over=(1, 0)):
    numbers = (((over[0],), (over[1],)), ((), ()))
    (a, b), (c, d) = halved(left), halved(right)
    passes = [lax.dot_general(x, y, numbers, preferred_element_type=jnp.float32) for x, y in ((a, d), (b, c), (a, c))]
    return passes[0] + passes[1] + passes[2]


def seats(position, round_index):
    upper = position + round_index
    upper = jnp.where(upper >= PERIOD, upper - PERIOD, upper)
    lower = round_index - (position - HALF)
    lower = jnp.where(lower < 0, lower + PERIOD, lower)
    return jnp.where(position < HALF, upper, jnp.where(position == HALF, PERIOD, lower))


def placing(round_index, swapped=None):
    index = lax.broadcasted_iota(jnp.int32, (N, N), 0)
    if swapped is not None:
        index = jnp.where(swapped, jnp.where(index < HALF, index + HALF, index - HALF), index)
    position = lax.broadcasted_iota(jnp.int32, (N, N), 1)
    return (index == seats(position, round_index)).astype(jnp.bfloat16)


def thirds(values):
    high = values.astype(jnp.bfloat16)
    rest = values - high.astype(jnp.float32)
    middle = rest.astype(jnp.bfloat16)
    return high, middle, (rest - middle.astype(jnp.float32)).astype(jnp.bfloat16)


def placed(pieces, place, over):
    numbers = (((1,), (over,)), ((), ()))
    return [lax.dot_general(x, place, numbers, preferred_element_type=jnp.float32) for x in pieces]


def laid_both(values, place, over):
    columns = [x.astype(jnp.bfloat16) for x in placed(thirds(values), place, over)]
    numbers = (((over,), (0,)), ((), ()))
    return sum(lax.dot_general(place, x, numbers, preferred_element_type=jnp.float32) for x in columns)


def rotations(upper_diag, coupling, lower_diag, round_index):
    position = lax.broadcasted_iota(jnp.int32, (1, HALF), 1)
    is_lower = seats(position, round_index) < seats(position + HALF, round_index)
    difference = jnp.where(is_lower, lower_diag - upper_diag, upper_diag - lower_diag)
    x = jnp.abs(difference)
    y = jnp.where(difference >= 0.0, 2.0 * coupling, -2.0 * coupling)
    largest = jnp.maximum(x, jnp.abs(y))
    scale = jnp.where(largest > 0.0, largest, 1.0)
    inverse = 1.0 / scale
    x = jnp.where(largest > 0.0, x * inverse, 1.0)
    y = y * inverse
    tangent = y / (x + jnp.sqrt(x * x + y * y))
    cosine = 1.0 / jnp.sqrt(1.0 + tangent * tangent)
    sine = tangent * cosine
    return cosine, jnp.where(is_lower, -sine, sine)


def turn(upper, lower, cosine, sine):
    return cosine * upper + sine * lower, cosine * lower - sine * upper


def shift(upper, lower, axis):
    at = lax.broadcasted_iota(jnp.int32, upper.shape, axis)
    new_upper = jnp.where(at == HALF - 1, lower, pltpu.roll(upper, HALF - 1, axis))
    moved = pltpu.roll(jnp.where(at == 0, upper, lower), 1, axis)
    return new_upper, jnp.where(at == 0, lower, moved)


def jacobi(gram, offset, second, parts):
    uu, ul, lu, ll, qu, ql = parts
    start = placing(offset)
    laid_out = laid_both(gram, start, 0)
    uu[...] = laid_out[:HALF, :HALF]
    ul[...] = laid_out[:HALF, HALF:]
    lu[...] = laid_out[HALF:, :HALF]
    ll[...] = laid_out[HALF:, HALF:]
    qu[...] = start[:, :HALF].astype(jnp.float32)
    ql[...] = start[:, HALF:].astype(jnp.float32)
    shape = (HALF, HALF)
    eye = lax.broadcasted_iota(jnp.int32, shape, 0) == lax.broadcasted_iota(jnp.int32, shape, 1)

    def diagonal(ref):
        return jnp.sum(jnp.where(eye, ref[...], 0.0), axis=0, keepdims=True)

    def stood(row):
        return jnp.sum(jnp.where(eye, jnp.broadcast_to(row, shape), 0.0), axis=1, keepdims=True)

    for round_index in range(offset, offset + ROUNDS):
        cosine, sine = rotations(diagonal(uu), diagonal(ul), diagonal(ll), round_index)
        cosine_col, sine_col = stood(cosine), stood(sine)
        a, b = shift(*turn(uu[...], ul[...], cosine, sine), 1)
        c, d = shift(*turn(lu[...], ll[...], cosine, sine), 1)
        uu[...], lu[...] = shift(*turn(a, c, cosine_col, sine_col), 0)
        ul[...], ll[...] = shift(*turn(b, d, cosine_col, sine_col), 0)
        qu[...], ql[...] = shift(*turn(qu[...], ql[...], cosine, sine), 1)
    end = placing(offset + ROUNDS, second == 0)
    rotation = sum(placed(thirds(jnp.concatenate([qu[...], ql[...]], axis=1)), end, 1))
    upper = jnp.concatenate([uu[...], ul[...]], axis=1)
    lower = jnp.concatenate([lu[...], ll[...]], axis=1)
    rotated_gram = laid_both(jnp.concatenate([upper, lower], axis=0), end, 1)
    return rotation, rotated_gram


def joined(kept_gram, cross, moved_gram):
    upper = jnp.concatenate([kept_gram, cross], axis=1)
    lower = jnp.concatenate([cross.T, moved_gram], axis=1)
    return jnp.concatenate([upper, lower], axis=0)


def tiles(square):
    sides = [square[:, :HALF].reshape(-1, 1, 8, HALF), square[:, HALF:].reshape(-1, 1, 8, HALF)]
    return jnp.concatenate(sides, axis=1)


def square_of(received, place):
    count, height = received.shape[0], TILES // received.shape[0] * 8
    part = received[:, place * height : (place + 1) * height, :].reshape(TILES // 2, 2, 8, HALF)
    return jnp.concatenate([part[:, 0].reshape(N, HALF), part[:, 1].reshape(N, HALF)], axis=1)


def pack_kernel(skipped, received, *refs):
    *blocks, out = refs
    count, height = out.shape[0], TILES // out.shape[0] * 8
    if received is not None:
        spread = received.shape[1] - skipped * height
        own = jnp.sum(received[:, skipped * height :, :], axis=0, keepdims=True)
        out[:, :spread, :] = jnp.broadcast_to(own, (count, spread, HALF))
    else:
        spread = 0
    for number, block in enumerate(blocks):
        at = spread + number * height
        out[:, at : at + height, :] = tiles(block[...]).reshape(count, height, HALF)


def step0_kernel(second, received, out, h0, *parts):
    q0, rotated_gram = jacobi(square_of(received, 0), 0, second[0, 0], parts)
    h0[...] = rotated_gram[:HALF, :HALF]
    out[:N] = q0
    out[N:] = rotated_gram[HALF:]


def step1_kernel(second, received, h0, out0, in0, out, carried, *parts):
    r1 = cross_dot(cross_dot(out0[:N], square_of(received, 1), (0, 0)), in0[:N])
    out[N:, HALF:] = r1[HALF:, HALF:]
    carried[:, HALF:] = r1[:, :HALF]
    gram = joined(h0[...], r1[:HALF, HALF:], in0[N:, HALF:])
    q1, h1 = jacobi(gram, ROUNDS, second[1, 0], parts)
    out[:N] = q1
    out[N:, :HALF] = h1[HALF:, HALF:]
    carried[:, :HALF] = h1[:, :HALF]


def cross2_kernel(received, out0, in0, q0_pp, out1, in1, carried, out, kept, gram):
    r2 = cross_dot(cross_dot(out0[:N], square_of(received, 0), (0, 0)), q0_pp[:N])
    upper = jnp.concatenate([carried[:HALF, HALF:], r2[:HALF, HALF:]], axis=1)
    lower = jnp.concatenate([in0[N:, :HALF], in1[N:, HALF:]], axis=1)
    s1 = cross_dot(cross_dot(out1[:N], jnp.concatenate([upper, lower], axis=0), (0, 0)), in1[:N])
    gram[...] = joined(carried[:HALF, :HALF], s1[:HALF, HALF:], in1[N:, :HALF])
    out[:HALF] = s1[HALF:, HALF:]
    out[HALF:N] = r2[HALF:, HALF:]
    out[N : N + HALF] = carried[HALF:, :HALF]
    out[N + HALF : 2 * N] = carried[HALF:, HALF:]
    out[2 * N : 3 * N] = in1[:N, HALF:]
    out[3 * N :] = q0_pp[:N, HALF:]
    kept[:HALF] = s1[:HALF, :HALF]
    kept[HALF:] = r2[:HALF, :HALF]


def step2_kernel(second, gram, out, own, *parts):
    q2, h2 = jacobi(gram[...], 2 * ROUNDS, second[2, 0], parts)
    out[:N] = q2[:, HALF:]
    out[N:] = h2[HALF:, HALF:]
    own[:N] = q2[:, :HALF]
    own[N:] = h2[:HALF, :HALF]


def shadow_kernel(received, in2a, kept, own2, out0, in0, q0_pp, out1, in1, *refs):
    x0, x1, x2, x3, left_of_cross, kept_cols, left_cols, right_cols, weights = refs
    q0_k, q1_k, q2_k = out0[:N, :HALF], out1[:N, :HALF], own2[:N]
    q1_pp, q0_ppp = in2a[2 * N : 3 * N], in2a[3 * N :]
    r3 = cross_dot(q0_k, cross_dot(square_of(received, 1), q0_ppp), (0, 0))
    upper = jnp.concatenate([kept[HALF:], r3], axis=1)
    lower = jnp.concatenate([in2a[N + HALF : 2 * N], in2a[HALF:N]], axis=1)
    t = cross_dot(q1_k, cross_dot(jnp.concatenate([upper, lower], axis=0), q1_pp), (0, 0))
    upper = jnp.concatenate([kept[:HALF], t], axis=1)
    lower = jnp.concatenate([in2a[N : N + HALF], in2a[:HALF]], axis=1)
    left_of_cross[...] = cross_dot(q2_k, jnp.concatenate([upper, lower], axis=0), (0, 0))

    q2_kk, q2_mk = own2[:HALF], own2[HALF:N]
    p1_kk, p1_mk, p1_km, p1_mm = in1[:HALF, :HALF], in1[HALF:N, :HALF], in1[:HALF, HALF:], in1[HALF:N, HALF:]
    weights[:, :HALF] = cross_dot(q0_k, cross_dot(out1[:HALF, :HALF], q2_kk))
    travelled = cross_dot(in0[:N, HALF:], cross_dot(out1[HALF:N, :HALF], q2_kk))
    weights[:, HALF:N] = travelled + cross_dot(in0[:N, :HALF], cross_dot(p1_km, q2_mk))
    weights[:, N : N + HALF] = cross_dot(in0[:N, :HALF], p1_kk)
    weights[:, N + HALF : 2 * N] = cross_dot(q0_pp[:N, HALF:], cross_dot(p1_mm, q2_mk))
    weights[:, 2 * N : 2 * N + HALF] = cross_dot(q0_pp[:N, HALF:], p1_mk)
    weights[:, 2 * N + HALF : 3 * N] = cross_dot(q0_pp[:N, :HALF], q1_pp[:HALF])
    weights[:, 3 * N :] = cross_dot(q0_ppp, q1_pp[HALF:])
    step = min(N, kept_cols.shape[0])

    def some_rows(number, carry):
        rows = pl.ds(pl.multiple_of(number * step, step), step)
        both = cross_dot(x1[rows, :], weights[:, HALF : N + HALF])
        three = cross_dot(x2[rows, :], weights[:, N + HALF : 3 * N])
        kept_cols[rows, :] = cross_dot(x0[rows, :], weights[:, :HALF]) + both[:, :HALF] + three[:, :HALF]
        left_cols[rows, :] = both[:, HALF:] + three[:, HALF:N]
        right_cols[rows, :] = three[:, N:] + cross_dot(x3[rows, :], weights[:, 3 * N :])
        return carry

    lax.fori_loop(0, kept_cols.shape[0] // step, some_rows, 0)


def last_kernel(place, kept_cols, left_cols, right_cols, in2b, q3, out):
    kept_weight, weight = q3[:HALF, place : place + HALF], q3[HALF:, place : place + HALF]
    left_weight, right_weight = cross_dot(in2b[:HALF], weight), cross_dot(in2b[HALF:N], weight)
    both = jnp.concatenate([kept_cols[...], left_cols[...]], axis=1)
    total = cross_dot(both, jnp.concatenate([kept_weight, left_weight], axis=0))
    out[...] = total + cross_dot(right_cols[...], right_weight)


def step3_kernel(second, left_of_cross, own2, in2b, q3, *parts):
    gram = joined(own2[N:], cross_dot(left_of_cross[...], in2b[:N]), in2b[N:])
    q3[...], _ = jacobi(gram, 3 * ROUNDS, second[3, 0], parts)


def products_kernel(left, right, out):
    step = min(N, left.shape[0])
    out[...] = jnp.zeros(out.shape, jnp.float32)

    def some_rows(number, carry):
        rows = pl.ds(pl.multiple_of(number * step, step), step)
        out[...] += cross_dot(left[rows, :], right[rows, :], (0, 0))
        return carry

    lax.fori_loop(0, left.shape[0] // step, some_rows, 0)


JACOBI_PARTS = [pltpu.VMEM((HALF, HALF), jnp.float32)] * 4 + [pltpu.VMEM((N, HALF), jnp.float32)] * 2


def run(kernel, shapes, *operands, last=(), scratch=()):
    whole, smem = pl.BlockSpec(memory_space=pltpu.VMEM), pl.BlockSpec(memory_space=pltpu.SMEM)
    specs = [smem if x.dtype == jnp.int32 else whole for x in operands]
    specs += [pl.BlockSpec(memory_space=pl.ANY)] * len(last)

    def body(*refs):
        kernel(*refs[: len(operands)], *refs[len(operands) + len(last) :])

    return pl.pallas_call(
        body,
        out_shape=[jax.ShapeDtypeStruct(shape, jnp.float32) for shape in shapes],
        in_specs=specs,
        out_specs=[whole] * len(shapes),
        scratch_shapes=scratch,
        compiler_params=pltpu.CompilerParams(vmem_limit_bytes=16 * 2**20),
        cost_estimate=pl.CostEstimate(flops=10**6, bytes_accessed=2**10, transcendentals=0),
    )(*operands, *last)


def shards(matrix, sender_slot):
    devices, count = lax.axis_size("blk"), lax.axis_size("row")

    def onward(values, places=1):
        return lax.ppermute(values, "blk", [((i - places) % devices, i) for i in range(devices)])

    def products(other):
        return run(products_kernel, [(N, N)], matrix, other)[0]

    def exchange(received, skipped, *blocks, last=()):
        height = TILES // count * 8
        given = [] if received is None else [received]
        total = len(blocks) * height + (0 if received is None else received.shape[1] - skipped * height)

        def kernel(*refs):
            pack_kernel(skipped, refs[0] if given else None, *refs[len(given) :])

        (pieces,) = run(kernel, [(count, total, HALF)], *given, *blocks, last=last)
        return lax.all_to_all(pieces, "row", 0, 0, tiled=True)

    square, block = (N, N), (HALF, HALF)
    before1, gram = lax.optimization_barrier((onward(matrix), products(matrix)))
    received = exchange(None, 0, gram, products(before1))
    before2, before3 = onward(before1), onward(before1, 2)
    with_c1 = exchange(received, 0, products(before2), products(before3))
    out0, h0 = run(step0_kernel, [(N + HALF, N), block], sender_slot, with_c1, scratch=JACOBI_PARTS)
    with_c3 = exchange(with_c1, 2)
    in0 = onward(out0)
    q0_pp = onward(in0)
    out1, carried = run(
        step1_kernel,
        [(N + HALF, N), square],
        *(sender_slot, with_c1, h0, out0, in0),
        scratch=JACOBI_PARTS,
    )
    in1 = onward(out1)
    out2a, kept, gram2 = run(
        cross2_kernel,
        [(4 * N, HALF), (N, HALF), square],
        *(with_c3, out0, in0, q0_pp, out1, in1, carried),
    )
    in2a = onward(out2a)
    out2b, own2 = run(step2_kernel, [(N + HALF, HALF)] * 2, sender_slot, gram2, scratch=JACOBI_PARTS)
    in2b = onward(out2b)
    rows = matrix.shape[0]
    left_of_cross, *columns = run(
        shadow_kernel,
        [(HALF, N)] + [(rows, HALF)] * 3,
        *(with_c3, in2a, kept, own2, out0, in0, q0_pp, out1, in1, matrix, before1, before2, before3),
        scratch=[pltpu.VMEM((N, 3 * N + HALF), jnp.float32)],
    )
    (q3,) = run(step3_kernel, [square], sender_slot, left_of_cross, own2, in2b, scratch=JACOBI_PARTS)

    def last_columns(place):
        return run(functools.partial(last_kernel, place), [(rows, HALF)], *columns, in2b, q3)[0]

    arrived = onward(last_columns(HALF))
    kept = last_columns(0)
    return jnp.concatenate([kept, arrived], axis=1)


def solution(mesh):
    return jax.shard_map(
        shards,
        mesh=mesh,
        in_specs=(P("row", "blk"), P(None, "blk")),
        out_specs=P("row", "blk"),
        check_vma=False,
    )
```

```python
import functools

import jax
import jax.numpy as jnp
from jax import lax
from jax.experimental import pallas as pl
from jax.experimental.pallas import tpu as pltpu
from jax.sharding import PartitionSpec as P

STEPS = 4
ROUNDS = 8
N = 256
HALF = 128
TILES = 64
PERIOD = N - 1


def dot(left, right, over=(1, 0), precision=lax.Precision.HIGHEST):
    return lax.dot_general(
        left,
        right,
        (((over[0],), (over[1],)), ((), ())),
        precision=precision,
        preferred_element_type=jnp.float32,
    )


def halved(values):
    high = values.astype(jnp.bfloat16)
    return high, (values - high.astype(jnp.float32)).astype(jnp.bfloat16)


def cross_dot(left, right, over=(1, 0)):
    numbers = (((over[0],), (over[1],)), ((), ()))
    (a, b), (c, d) = halved(left), halved(right)
    passes = [lax.dot_general(x, y, numbers, preferred_element_type=jnp.float32) for x, y in ((a, d), (b, c), (a, c))]
    return passes[0] + passes[1] + passes[2]


def seats(position, round_index):
    upper = position + round_index
    upper = jnp.where(upper >= PERIOD, upper - PERIOD, upper)
    lower = round_index - (position - HALF)
    lower = jnp.where(lower < 0, lower + PERIOD, lower)
    return jnp.where(position < HALF, upper, jnp.where(position == HALF, PERIOD, lower))


def placing(round_index, swapped=None):
    index = lax.broadcasted_iota(jnp.int32, (N, N), 0)
    if swapped is not None:
        index = jnp.where(swapped, jnp.where(index < HALF, index + HALF, index - HALF), index)
    position = lax.broadcasted_iota(jnp.int32, (N, N), 1)
    return (index == seats(position, round_index)).astype(jnp.bfloat16)


def thirds(values):
    high = values.astype(jnp.bfloat16)
    rest = values - high.astype(jnp.float32)
    middle = rest.astype(jnp.bfloat16)
    return high, middle, (rest - middle.astype(jnp.float32)).astype(jnp.bfloat16)


def placed(pieces, place, over):
    numbers = (((1,), (over,)), ((), ()))
    return [lax.dot_general(x, place, numbers, preferred_element_type=jnp.float32) for x in pieces]


def laid_both(values, place, over):
    columns = [x.astype(jnp.bfloat16) for x in placed(thirds(values), place, over)]
    numbers = (((over,), (0,)), ((), ()))
    return sum(lax.dot_general(place, x, numbers, preferred_element_type=jnp.float32) for x in columns)


def rotations(upper_diag, coupling, lower_diag, round_index):
    position = lax.broadcasted_iota(jnp.int32, (1, HALF), 1)
    is_lower = seats(position, round_index) < seats(position + HALF, round_index)
    difference = jnp.where(is_lower, lower_diag - upper_diag, upper_diag - lower_diag)
    x = jnp.abs(difference)
    y = jnp.where(difference >= 0.0, 2.0 * coupling, -2.0 * coupling)
    largest = jnp.maximum(x, jnp.abs(y))
    scale = jnp.where(largest > 0.0, largest, 1.0)
    inverse = 1.0 / scale
    x = jnp.where(largest > 0.0, x * inverse, 1.0)
    y = y * inverse
    tangent = y / (x + jnp.sqrt(x * x + y * y))
    cosine = 1.0 / jnp.sqrt(1.0 + tangent * tangent)
    sine = tangent * cosine
    return cosine, jnp.where(is_lower, -sine, sine)


def turn(upper, lower, cosine, sine):
    return cosine * upper + sine * lower, cosine * lower - sine * upper


def shift(upper, lower, axis):
    at = lax.broadcasted_iota(jnp.int32, upper.shape, axis)
    new_upper = jnp.where(at == HALF - 1, lower, pltpu.roll(upper, HALF - 1, axis))
    moved = pltpu.roll(jnp.where(at == 0, upper, lower), 1, axis)
    return new_upper, jnp.where(at == 0, lower, moved)


def jacobi(gram, offset, second, parts):
    uu, ul, lu, ll, qu, ql = parts
    start = placing(offset)
    laid_out = laid_both(gram, start, 0)
    uu[...] = laid_out[:HALF, :HALF]
    ul[...] = laid_out[:HALF, HALF:]
    lu[...] = laid_out[HALF:, :HALF]
    ll[...] = laid_out[HALF:, HALF:]
    qu[...] = start[:, :HALF].astype(jnp.float32)
    ql[...] = start[:, HALF:].astype(jnp.float32)
    shape = (HALF, HALF)
    eye = lax.broadcasted_iota(jnp.int32, shape, 0) == lax.broadcasted_iota(jnp.int32, shape, 1)

    def diagonal(ref):
        return jnp.sum(jnp.where(eye, ref[...], 0.0), axis=0, keepdims=True)

    def stood(row):
        return jnp.sum(jnp.where(eye, jnp.broadcast_to(row, shape), 0.0), axis=1, keepdims=True)

    for round_index in range(offset, offset + ROUNDS):
        cosine, sine = rotations(diagonal(uu), diagonal(ul), diagonal(ll), round_index)
        cosine_col, sine_col = stood(cosine), stood(sine)
        a, b = shift(*turn(uu[...], ul[...], cosine, sine), 1)
        c, d = shift(*turn(lu[...], ll[...], cosine, sine), 1)
        uu[...], lu[...] = shift(*turn(a, c, cosine_col, sine_col), 0)
        ul[...], ll[...] = shift(*turn(b, d, cosine_col, sine_col), 0)
        qu[...], ql[...] = shift(*turn(qu[...], ql[...], cosine, sine), 1)
    end = placing(offset + ROUNDS, second == 0)
    rotation = sum(placed(thirds(jnp.concatenate([qu[...], ql[...]], axis=1)), end, 1))
    upper = jnp.concatenate([uu[...], ul[...]], axis=1)
    lower = jnp.concatenate([lu[...], ll[...]], axis=1)
    rotated_gram = laid_both(jnp.concatenate([upper, lower], axis=0), end, 1)
    return rotation, rotated_gram


def joined(kept_gram, cross, moved_gram):
    upper = jnp.concatenate([kept_gram, cross], axis=1)
    lower = jnp.concatenate([cross.T, moved_gram], axis=1)
    return jnp.concatenate([upper, lower], axis=0)


def tiles(square):
    sides = [square[:, :HALF].reshape(-1, 1, 8, HALF), square[:, HALF:].reshape(-1, 1, 8, HALF)]
    return jnp.concatenate(sides, axis=1)


def square_of(received, place):
    count, height = received.shape[0], TILES // received.shape[0] * 8
    part = received[:, place * height : (place + 1) * height, :].reshape(TILES // 2, 2, 8, HALF)
    return jnp.concatenate([part[:, 0].reshape(N, HALF), part[:, 1].reshape(N, HALF)], axis=1)


def pack_kernel(skipped, received, *refs):
    *blocks, out = refs
    count, height = out.shape[0], TILES // out.shape[0] * 8
    if received is not None:
        spread = received.shape[1] - skipped * height
        own = jnp.sum(received[:, skipped * height :, :], axis=0, keepdims=True)
        out[:, :spread, :] = jnp.broadcast_to(own, (count, spread, HALF))
    else:
        spread = 0
    for number, block in enumerate(blocks):
        at = spread + number * height
        out[:, at : at + height, :] = tiles(block[...]).reshape(count, height, HALF)


def step0_kernel(second, received, out, h0, *parts):
    q0, rotated_gram = jacobi(square_of(received, 0), 0, second[0, 0], parts)
    h0[...] = rotated_gram[:HALF, :HALF]
    out[:N] = q0
    out[N:] = rotated_gram[HALF:]


def step1_kernel(second, received, h0, out0, in0, out, carried, *parts):
    q0_p = in0[:N]
    r1 = cross_dot(cross_dot(out0[:N], square_of(received, 1), (0, 0)), q0_p)
    out[N + HALF : 2 * N] = r1[HALF:]
    out[2 * N :] = q0_p
    carried[:, HALF:] = r1[:HALF, :HALF]
    q1, h1 = jacobi(joined(h0[...], r1[:HALF, HALF:], in0[N:, HALF:]), ROUNDS, second[1, 0], parts)
    out[:N] = q1
    out[N : N + HALF] = h1[HALF:]
    carried[:, :HALF] = h1[:HALF, :HALF]


def cross2_kernel(received, out0, in0, out1, in1, carried, out, kept, gram):
    q0_pp = in1[2 * N :]
    r2 = cross_dot(cross_dot(out0[:N], square_of(received, 0), (0, 0)), q0_pp)
    upper = jnp.concatenate([carried[:, HALF:], r2[:HALF, HALF:]], axis=1)
    lower = jnp.concatenate([in0[N:, :HALF], in1[N + HALF : 2 * N, HALF:]], axis=1)
    s1 = cross_dot(cross_dot(out1[:N], jnp.concatenate([upper, lower], axis=0), (0, 0)), in1[:N])
    gram[...] = joined(carried[:, :HALF], s1[:HALF, HALF:], in1[N : N + HALF, HALF:])
    out[:HALF] = s1[HALF:, HALF:]
    out[HALF:N] = r2[HALF:, HALF:]
    out[N : 2 * N] = in1[:N, HALF:]
    out[2 * N :] = q0_pp[:, HALF:]
    kept[:HALF] = s1[:HALF, :HALF]
    kept[HALF:] = r2[:HALF, :HALF]


def step2_kernel(second, gram, out, own, *parts):
    q2, h2 = jacobi(gram[...], 2 * ROUNDS, second[2, 0], parts)
    out[:N] = q2[:, HALF:]
    out[N:] = h2[HALF:, HALF:]
    own[:N] = q2[:, :HALF]
    own[N:] = h2[:HALF, :HALF]


def in_chunks(count, some_rows):
    step = min(N, count)

    def one(number, carry):
        some_rows(pl.ds(pl.multiple_of(number * step, step), step))
        return carry

    lax.fori_loop(0, count // step, one, 0)


def columns_kernel(out0, in0, out1, in1, own2, x0, x1, x2, kept_cols, left_cols, weights):
    q2_kk, q2_mk, q0_pp = own2[:HALF], own2[HALF:N], in1[2 * N :]
    p1_kk, p1_mk, p1_km, p1_mm = in1[:HALF, :HALF], in1[HALF:N, :HALF], in1[:HALF, HALF:], in1[HALF:N, HALF:]
    weights[:, :HALF] = cross_dot(out0[:N, :HALF], cross_dot(out1[:HALF, :HALF], q2_kk))
    travelled = cross_dot(in0[:N, HALF:], cross_dot(out1[HALF:N, :HALF], q2_kk))
    weights[:, HALF:N] = travelled + cross_dot(in0[:N, :HALF], cross_dot(p1_km, q2_mk))
    weights[:, N : N + HALF] = cross_dot(in0[:N, :HALF], p1_kk)
    weights[:, N + HALF : 2 * N] = cross_dot(q0_pp[:, HALF:], cross_dot(p1_mm, q2_mk))
    weights[:, 2 * N :] = cross_dot(q0_pp[:, HALF:], p1_mk)

    def some_rows(rows):
        both = cross_dot(x1[rows, :], weights[:, HALF : N + HALF]) + cross_dot(x2[rows, :], weights[:, N + HALF :])
        kept_cols[rows, :] = cross_dot(x0[rows, :], weights[:, :HALF]) + both[:, :HALF]
        left_cols[rows, :] = both[:, HALF:]

    in_chunks(kept_cols.shape[0], some_rows)


def cross3_kernel(received, out0, out1, in1, in2a, kept, own2, x2, x3, left_of_cross, right_cols, weights):
    q0_k, q1_k, q2_k = out0[:N, :HALF], out1[:N, :HALF], own2[:N]
    q1_pp, q0_ppp = in2a[N : 2 * N], in2a[2 * N :]
    r3 = cross_dot(q0_k, cross_dot(square_of(received, 0), q0_ppp), (0, 0))
    upper = jnp.concatenate([kept[HALF:], r3], axis=1)
    lower = jnp.concatenate([in1[N + HALF : 2 * N, :HALF], in2a[HALF:N]], axis=1)
    t = cross_dot(q1_k, cross_dot(jnp.concatenate([upper, lower], axis=0), q1_pp), (0, 0))
    upper = jnp.concatenate([kept[:HALF], t], axis=1)
    lower = jnp.concatenate([in1[N : N + HALF, :HALF], in2a[:HALF]], axis=1)
    left_of_cross[...] = cross_dot(q2_k, jnp.concatenate([upper, lower], axis=0), (0, 0))
    weights[:, :HALF] = cross_dot(in1[2 * N :, :HALF], q1_pp[:HALF])
    weights[:, HALF:] = cross_dot(q0_ppp, q1_pp[HALF:])

    def some_rows(rows):
        right_cols[rows, :] = cross_dot(x2[rows, :], weights[:, :HALF]) + cross_dot(x3[rows, :], weights[:, HALF:])

    in_chunks(right_cols.shape[0], some_rows)


def last_kernel(place, kept_cols, left_cols, right_cols, in2b, q3, out):
    kept_weight, weight = q3[:HALF, place : place + HALF], q3[HALF:, place : place + HALF]
    left_weight, right_weight = cross_dot(in2b[:HALF], weight), cross_dot(in2b[HALF:N], weight)
    both = jnp.concatenate([kept_cols[...], left_cols[...]], axis=1)
    total = cross_dot(both, jnp.concatenate([kept_weight, left_weight], axis=0))
    out[...] = total + cross_dot(right_cols[...], right_weight)


def step3_kernel(second, left_of_cross, own2, in2b, q3, *parts):
    gram = joined(own2[N:], cross_dot(left_of_cross[...], in2b[:N]), in2b[N:])
    q3[...], _ = jacobi(gram, 3 * ROUNDS, second[3, 0], parts)


def products_kernel(left, right, out):
    out[...] = jnp.zeros(out.shape, jnp.float32)

    def some_rows(rows):
        out[...] += cross_dot(left[rows, :], right[rows, :], (0, 0))

    in_chunks(left.shape[0], some_rows)


JACOBI_PARTS = [pltpu.VMEM((HALF, HALF), jnp.float32)] * 4 + [pltpu.VMEM((N, HALF), jnp.float32)] * 2


def run(kernel, shapes, *operands, last=(), scratch=()):
    whole, smem = pl.BlockSpec(memory_space=pltpu.VMEM), pl.BlockSpec(memory_space=pltpu.SMEM)
    specs = [smem if x.dtype == jnp.int32 else whole for x in operands]
    specs += [pl.BlockSpec(memory_space=pl.ANY)] * len(last)

    def body(*refs):
        kernel(*refs[: len(operands)], *refs[len(operands) + len(last) :])

    return pl.pallas_call(
        body,
        out_shape=[jax.ShapeDtypeStruct(shape, jnp.float32) for shape in shapes],
        in_specs=specs,
        out_specs=[whole] * len(shapes),
        scratch_shapes=scratch,
        compiler_params=pltpu.CompilerParams(vmem_limit_bytes=16 * 2**20),
        cost_estimate=pl.CostEstimate(flops=10**6, bytes_accessed=2**10, transcendentals=0),
    )(*operands, *last)


def shards(matrix, sender_slot):
    devices, count = lax.axis_size("blk"), lax.axis_size("row")

    def onward(values, places=1):
        return lax.ppermute(values, "blk", [((i - places) % devices, i) for i in range(devices)])

    def products(other):
        return run(products_kernel, [(N, N)], matrix, other)[0]

    def exchange(received, skipped, *blocks, last=()):
        height = TILES // count * 8
        given = [] if received is None else [received]
        total = len(blocks) * height + (0 if received is None else received.shape[1] - skipped * height)

        def kernel(*refs):
            pack_kernel(skipped, refs[0] if given else None, *refs[len(given) :])

        (pieces,) = run(kernel, [(count, total, HALF)], *given, *blocks, last=last)
        return lax.all_to_all(pieces, "row", 0, 0, tiled=True)

    square, block = (N, N), (HALF, HALF)
    before1, gram = lax.optimization_barrier((onward(matrix), products(matrix)))
    received = exchange(None, 0, gram, products(before1))
    before2 = onward(before1)
    with_c1 = exchange(received, 0, products(before2))
    before3 = onward(before2)
    with_c2 = exchange(with_c1, 2, products(before3))
    out0, h0 = run(step0_kernel, [(N + HALF, N), block], sender_slot, with_c1, scratch=JACOBI_PARTS)
    in0 = onward(out0)
    out1, carried = run(
        step1_kernel,
        [(3 * N, N), (HALF, N)],
        *(sender_slot, with_c1, h0, out0, in0),
        scratch=JACOBI_PARTS,
    )
    in1 = onward(out1)
    with_c3 = exchange(with_c2, 1, last=(out1,))
    out2a, kept, gram2 = run(
        cross2_kernel,
        [(3 * N, HALF), (N, HALF), square],
        *(with_c2, out0, in0, out1, in1, carried),
    )
    in2a = onward(out2a)
    out2b, own2 = run(step2_kernel, [(N + HALF, HALF)] * 2, sender_slot, gram2, scratch=JACOBI_PARTS)
    in2b = onward(out2b)
    rows = matrix.shape[0]
    kept_cols, left_cols = run(
        columns_kernel,
        [(rows, HALF)] * 2,
        *(out0, in0, out1, in1, own2, matrix, before1, before2),
        scratch=[pltpu.VMEM((N, 2 * N + HALF), jnp.float32)],
    )
    left_of_cross, right_cols = run(
        cross3_kernel,
        [(HALF, N), (rows, HALF)],
        *(with_c3, out0, out1, in1, in2a, kept, own2, before2, before3),
        scratch=[pltpu.VMEM((N, N), jnp.float32)],
        last=(kept_cols,),
    )
    columns = (kept_cols, left_cols, right_cols)
    (q3,) = run(step3_kernel, [square], sender_slot, left_of_cross, own2, in2b, scratch=JACOBI_PARTS)

    def last_columns(place):
        return run(functools.partial(last_kernel, place), [(rows, HALF)], *columns, in2b, q3)[0]

    arrived = onward(last_columns(HALF))
    kept = last_columns(0)
    return jnp.concatenate([kept, arrived], axis=1)


def solution(mesh):
    return jax.shard_map(
        shards,
        mesh=mesh,
        in_specs=(P("row", "blk"), P(None, "blk")),
        out_specs=P("row", "blk"),
        check_vma=False,
    )
```

```python
import functools

import jax
import jax.numpy as jnp
from jax import lax
from jax.experimental import pallas as pl
from jax.experimental.pallas import tpu as pltpu
from jax.sharding import PartitionSpec as P

STEPS = 4
ROUNDS = 8
N = 256
HALF = 128
TILES = 64
PERIOD = N - 1


def dot(left, right, over=(1, 0), precision=lax.Precision.HIGHEST):
    return lax.dot_general(
        left,
        right,
        (((over[0],), (over[1],)), ((), ())),
        precision=precision,
        preferred_element_type=jnp.float32,
    )


def halved(values):
    high = values.astype(jnp.bfloat16)
    return high, (values - high.astype(jnp.float32)).astype(jnp.bfloat16)


def cross_dot(left, right, over=(1, 0)):
    numbers = (((over[0],), (over[1],)), ((), ()))
    (a, b), (c, d) = halved(left), halved(right)
    passes = [lax.dot_general(x, y, numbers, preferred_element_type=jnp.float32) for x, y in ((a, d), (b, c), (a, c))]
    return passes[0] + passes[1] + passes[2]


def seats(position, round_index):
    upper = position + round_index
    upper = jnp.where(upper >= PERIOD, upper - PERIOD, upper)
    lower = round_index - (position - HALF)
    lower = jnp.where(lower < 0, lower + PERIOD, lower)
    return jnp.where(position < HALF, upper, jnp.where(position == HALF, PERIOD, lower))


def placing(round_index, swapped=None):
    index = lax.broadcasted_iota(jnp.int32, (N, N), 0)
    if swapped is not None:
        index = jnp.where(swapped, jnp.where(index < HALF, index + HALF, index - HALF), index)
    position = lax.broadcasted_iota(jnp.int32, (N, N), 1)
    return (index == seats(position, round_index)).astype(jnp.bfloat16)


def thirds(values):
    high = values.astype(jnp.bfloat16)
    rest = values - high.astype(jnp.float32)
    middle = rest.astype(jnp.bfloat16)
    return high, middle, (rest - middle.astype(jnp.float32)).astype(jnp.bfloat16)


def placed(pieces, place, over):
    numbers = (((1,), (over,)), ((), ()))
    return [lax.dot_general(x, place, numbers, preferred_element_type=jnp.float32) for x in pieces]


def laid_both(values, place, over):
    columns = [x.astype(jnp.bfloat16) for x in placed(thirds(values), place, over)]
    numbers = (((over,), (0,)), ((), ()))
    return sum(lax.dot_general(place, x, numbers, preferred_element_type=jnp.float32) for x in columns)


def rotations(upper_diag, coupling, lower_diag, round_index):
    position = lax.broadcasted_iota(jnp.int32, (1, HALF), 1)
    is_lower = seats(position, round_index) < seats(position + HALF, round_index)
    difference = jnp.where(is_lower, lower_diag - upper_diag, upper_diag - lower_diag)
    x = jnp.abs(difference)
    y = jnp.where(difference >= 0.0, 2.0 * coupling, -2.0 * coupling)
    largest = jnp.maximum(x, jnp.abs(y))
    scale = jnp.where(largest > 0.0, largest, 1.0)
    inverse = 1.0 / scale
    x = jnp.where(largest > 0.0, x * inverse, 1.0)
    y = y * inverse
    tangent = y / (x + jnp.sqrt(x * x + y * y))
    cosine = 1.0 / jnp.sqrt(1.0 + tangent * tangent)
    sine = tangent * cosine
    return cosine, jnp.where(is_lower, -sine, sine)


def turn(upper, lower, cosine, sine):
    return cosine * upper + sine * lower, cosine * lower - sine * upper


def shift(upper, lower, axis):
    at = lax.broadcasted_iota(jnp.int32, upper.shape, axis)
    new_upper = jnp.where(at == HALF - 1, lower, pltpu.roll(upper, HALF - 1, axis))
    moved = pltpu.roll(jnp.where(at == 0, upper, lower), 1, axis)
    return new_upper, jnp.where(at == 0, lower, moved)


def jacobi(gram, offset, second, parts):
    uu, ul, lu, ll, qu, ql = parts
    start = placing(offset)
    laid_out = laid_both(gram, start, 0)
    uu[...] = laid_out[:HALF, :HALF]
    ul[...] = laid_out[:HALF, HALF:]
    lu[...] = laid_out[HALF:, :HALF]
    ll[...] = laid_out[HALF:, HALF:]
    qu[...] = start[:, :HALF].astype(jnp.float32)
    ql[...] = start[:, HALF:].astype(jnp.float32)
    shape = (HALF, HALF)
    eye = lax.broadcasted_iota(jnp.int32, shape, 0) == lax.broadcasted_iota(jnp.int32, shape, 1)

    def diagonal(ref):
        return jnp.sum(jnp.where(eye, ref[...], 0.0), axis=0, keepdims=True)

    def stood(row):
        return jnp.sum(jnp.where(eye, jnp.broadcast_to(row, shape), 0.0), axis=1, keepdims=True)

    for round_index in range(offset, offset + ROUNDS):
        cosine, sine = rotations(diagonal(uu), diagonal(ul), diagonal(ll), round_index)
        cosine_col, sine_col = stood(cosine), stood(sine)
        a, b = shift(*turn(uu[...], ul[...], cosine, sine), 1)
        c, d = shift(*turn(lu[...], ll[...], cosine, sine), 1)
        uu[...], lu[...] = shift(*turn(a, c, cosine_col, sine_col), 0)
        ul[...], ll[...] = shift(*turn(b, d, cosine_col, sine_col), 0)
        qu[...], ql[...] = shift(*turn(qu[...], ql[...], cosine, sine), 1)
    end = placing(offset + ROUNDS, second == 0)
    rotation = sum(placed(thirds(jnp.concatenate([qu[...], ql[...]], axis=1)), end, 1))
    upper = jnp.concatenate([uu[...], ul[...]], axis=1)
    lower = jnp.concatenate([lu[...], ll[...]], axis=1)
    rotated_gram = laid_both(jnp.concatenate([upper, lower], axis=0), end, 1)
    return rotation, rotated_gram


def joined(kept_gram, cross, moved_gram):
    upper = jnp.concatenate([kept_gram, cross], axis=1)
    lower = jnp.concatenate([cross.T, moved_gram], axis=1)
    return jnp.concatenate([upper, lower], axis=0)


def tiles(square):
    sides = [square[:, :HALF].reshape(-1, 1, 8, HALF), square[:, HALF:].reshape(-1, 1, 8, HALF)]
    return jnp.concatenate(sides, axis=1)


def square_of(received, place):
    count, height = received.shape[0], TILES // received.shape[0] * 8
    part = received[:, place * height : (place + 1) * height, :].reshape(TILES // 2, 2, 8, HALF)
    return jnp.concatenate([part[:, 0].reshape(N, HALF), part[:, 1].reshape(N, HALF)], axis=1)


def pack_kernel(skipped, received, *refs):
    *blocks, out = refs
    count, height = out.shape[0], TILES // out.shape[0] * 8
    if received is not None:
        spread = received.shape[1] - skipped * height
        own = jnp.sum(received[:, skipped * height :, :], axis=0, keepdims=True)
        out[:, :spread, :] = jnp.broadcast_to(own, (count, spread, HALF))
    else:
        spread = 0
    for number, block in enumerate(blocks):
        at = spread + number * height
        out[:, at : at + height, :] = tiles(block[...]).reshape(count, height, HALF)


def step0_kernel(second, received, out, h0, *parts):
    q0, rotated_gram = jacobi(square_of(received, 0), 0, second[0, 0], parts)
    h0[...] = rotated_gram[:HALF, :HALF]
    out[:N] = q0
    out[N:] = rotated_gram[HALF:]


def step1_kernel(second, received, h0, out0, in0, out, carried, *parts):
    q0_p = in0[:N]
    r1 = cross_dot(cross_dot(out0[:N], square_of(received, 1), (0, 0)), q0_p)
    out[N + HALF : 2 * N] = r1[HALF:]
    out[2 * N :] = q0_p
    carried[:, HALF:] = r1[:HALF, :HALF]
    q1, h1 = jacobi(joined(h0[...], r1[:HALF, HALF:], in0[N:, HALF:]), ROUNDS, second[1, 0], parts)
    out[:N] = q1
    out[N : N + HALF] = h1[HALF:]
    carried[:, :HALF] = h1[:HALF, :HALF]


def cross2_kernel(received, out0, in0, out1, in1, carried, out, kept, gram):
    q0_pp = in1[2 * N :]
    r2 = cross_dot(cross_dot(out0[:N], square_of(received, 0), (0, 0)), q0_pp)
    upper = jnp.concatenate([carried[:, HALF:], r2[:HALF, HALF:]], axis=1)
    lower = jnp.concatenate([in0[N:, :HALF], in1[N + HALF : 2 * N, HALF:]], axis=1)
    s1 = cross_dot(cross_dot(out1[:N], jnp.concatenate([upper, lower], axis=0), (0, 0)), in1[:N])
    gram[...] = joined(carried[:, :HALF], s1[:HALF, HALF:], in1[N : N + HALF, HALF:])
    out[:HALF] = s1[HALF:, HALF:]
    out[HALF:N] = r2[HALF:, HALF:]
    out[N : 2 * N] = in1[:N, HALF:]
    out[2 * N :] = q0_pp[:, HALF:]
    kept[:HALF] = s1[:HALF, :HALF]
    kept[HALF:] = r2[:HALF, :HALF]


def step2_kernel(second, gram, out, own, *parts):
    q2, h2 = jacobi(gram[...], 2 * ROUNDS, second[2, 0], parts)
    out[:N] = q2[:, HALF:]
    out[N:] = h2[HALF:, HALF:]
    own[:N] = q2[:, :HALF]
    own[N:] = h2[:HALF, :HALF]


def in_chunks(count, some_rows):
    step = min(N, count)

    def one(number, carry):
        some_rows(pl.ds(pl.multiple_of(number * step, step), step))
        return carry

    lax.fori_loop(0, count // step, one, 0)


def shadow_kernel(received, out0, in0, out1, in1, in2a, kept, own2, x0, x1, x2, x3, *refs):
    left_of_cross, kept_cols, left_cols, right_cols, weights = refs
    q0_k, q1_k, q2_k, q0_pp = out0[:N, :HALF], out1[:N, :HALF], own2[:N], in1[2 * N :]
    q1_pp, q0_ppp = in2a[N : 2 * N], in2a[2 * N :]
    r3 = cross_dot(q0_k, cross_dot(square_of(received, 0), q0_ppp), (0, 0))
    upper = jnp.concatenate([kept[HALF:], r3], axis=1)
    lower = jnp.concatenate([in1[N + HALF : 2 * N, :HALF], in2a[HALF:N]], axis=1)
    t = cross_dot(q1_k, cross_dot(jnp.concatenate([upper, lower], axis=0), q1_pp), (0, 0))
    upper = jnp.concatenate([kept[:HALF], t], axis=1)
    lower = jnp.concatenate([in1[N : N + HALF, :HALF], in2a[:HALF]], axis=1)
    left_of_cross[...] = cross_dot(q2_k, jnp.concatenate([upper, lower], axis=0), (0, 0))

    q2_kk, q2_mk = own2[:HALF], own2[HALF:N]
    p1_kk, p1_mk, p1_km, p1_mm = in1[:HALF, :HALF], in1[HALF:N, :HALF], in1[:HALF, HALF:], in1[HALF:N, HALF:]
    weights[:, :HALF] = cross_dot(q0_k, cross_dot(out1[:HALF, :HALF], q2_kk))
    travelled = cross_dot(in0[:N, HALF:], cross_dot(out1[HALF:N, :HALF], q2_kk))
    weights[:, HALF:N] = travelled + cross_dot(in0[:N, :HALF], cross_dot(p1_km, q2_mk))
    weights[:, N : N + HALF] = cross_dot(in0[:N, :HALF], p1_kk)
    weights[:, N + HALF : 2 * N] = cross_dot(q0_pp[:, HALF:], cross_dot(p1_mm, q2_mk))
    weights[:, 2 * N : 2 * N + HALF] = cross_dot(q0_pp[:, HALF:], p1_mk)
    weights[:, 2 * N + HALF : 3 * N] = cross_dot(q0_pp[:, :HALF], q1_pp[:HALF])
    weights[:, 3 * N :] = cross_dot(q0_ppp, q1_pp[HALF:])

    def some_rows(rows):
        both = cross_dot(x1[rows, :], weights[:, HALF : N + HALF])
        three = cross_dot(x2[rows, :], weights[:, N + HALF : 3 * N])
        kept_cols[rows, :] = cross_dot(x0[rows, :], weights[:, :HALF]) + both[:, :HALF] + three[:, :HALF]
        left_cols[rows, :] = both[:, HALF:] + three[:, HALF:N]
        right_cols[rows, :] = three[:, N:] + cross_dot(x3[rows, :], weights[:, 3 * N :])

    in_chunks(kept_cols.shape[0], some_rows)


def last_kernel(place, kept_cols, left_cols, right_cols, in2b, q3, out):
    kept_weight, weight = q3[:HALF, place : place + HALF], q3[HALF:, place : place + HALF]
    left_weight, right_weight = cross_dot(in2b[:HALF], weight), cross_dot(in2b[HALF:N], weight)
    both = jnp.concatenate([kept_cols[...], left_cols[...]], axis=1)
    total = cross_dot(both, jnp.concatenate([kept_weight, left_weight], axis=0))
    out[...] = total + cross_dot(right_cols[...], right_weight)


def step3_kernel(second, left_of_cross, own2, in2b, q3, *parts):
    gram = joined(own2[N:], cross_dot(left_of_cross[...], in2b[:N]), in2b[N:])
    q3[...], _ = jacobi(gram, 3 * ROUNDS, second[3, 0], parts)


def products_kernel(left, right, out):
    out[...] = jnp.zeros(out.shape, jnp.float32)

    def some_rows(rows):
        out[...] += cross_dot(left[rows, :], right[rows, :], (0, 0))

    in_chunks(left.shape[0], some_rows)


JACOBI_PARTS = [pltpu.VMEM((HALF, HALF), jnp.float32)] * 4 + [pltpu.VMEM((N, HALF), jnp.float32)] * 2


def run(kernel, shapes, *operands, last=(), scratch=()):
    whole, smem = pl.BlockSpec(memory_space=pltpu.VMEM), pl.BlockSpec(memory_space=pltpu.SMEM)
    specs = [smem if x.dtype == jnp.int32 else whole for x in operands]
    specs += [pl.BlockSpec(memory_space=pl.ANY)] * len(last)

    def body(*refs):
        kernel(*refs[: len(operands)], *refs[len(operands) + len(last) :])

    return pl.pallas_call(
        body,
        out_shape=[jax.ShapeDtypeStruct(shape, jnp.float32) for shape in shapes],
        in_specs=specs,
        out_specs=[whole] * len(shapes),
        scratch_shapes=scratch,
        compiler_params=pltpu.CompilerParams(vmem_limit_bytes=16 * 2**20),
        cost_estimate=pl.CostEstimate(flops=10**6, bytes_accessed=2**10, transcendentals=0),
    )(*operands, *last)


def shards(matrix, sender_slot):
    devices, count = lax.axis_size("blk"), lax.axis_size("row")

    def onward(values, places=1):
        return lax.ppermute(values, "blk", [((i - places) % devices, i) for i in range(devices)])

    def products(other):
        return run(products_kernel, [(N, N)], matrix, other)[0]

    def exchange(received, skipped, *blocks, last=()):
        height = TILES // count * 8
        given = [] if received is None else [received]
        total = len(blocks) * height + (0 if received is None else received.shape[1] - skipped * height)

        def kernel(*refs):
            pack_kernel(skipped, refs[0] if given else None, *refs[len(given) :])

        (pieces,) = run(kernel, [(count, total, HALF)], *given, *blocks, last=last)
        return lax.all_to_all(pieces, "row", 0, 0, tiled=True)

    square, block = (N, N), (HALF, HALF)
    before1, gram = lax.optimization_barrier((onward(matrix), products(matrix)))
    received = exchange(None, 0, gram, products(before1))
    before2 = onward(before1)
    with_c1 = exchange(received, 0, products(before2))
    before3 = onward(before2)
    parts3 = products(before3)
    with_c2 = exchange(with_c1, 2, parts3)
    out0, h0 = run(
        step0_kernel, [(N + HALF, N), block], sender_slot, with_c1, scratch=JACOBI_PARTS, last=(parts3,)
    )
    in0 = onward(out0)
    out1, carried = run(
        step1_kernel,
        [(3 * N, N), (HALF, N)],
        *(sender_slot, with_c1, h0, out0, in0),
        scratch=JACOBI_PARTS,
    )
    in1 = onward(out1)
    with_c3 = exchange(with_c2, 1, last=(out1,))
    out2a, kept, gram2 = run(
        cross2_kernel,
        [(3 * N, HALF), (N, HALF), square],
        *(with_c2, out0, in0, out1, in1, carried),
    )
    in2a = onward(out2a)
    out2b, own2 = run(step2_kernel, [(N + HALF, HALF)] * 2, sender_slot, gram2, scratch=JACOBI_PARTS)
    in2b = onward(out2b)
    rows = matrix.shape[0]
    left_of_cross, *columns = run(
        shadow_kernel,
        [(HALF, N)] + [(rows, HALF)] * 3,
        *(with_c3, out0, in0, out1, in1, in2a, kept, own2, matrix, before1, before2, before3),
        scratch=[pltpu.VMEM((N, 3 * N + HALF), jnp.float32)],
    )
    (q3,) = run(step3_kernel, [square], sender_slot, left_of_cross, own2, in2b, scratch=JACOBI_PARTS)

    def last_columns(place):
        return run(functools.partial(last_kernel, place), [(rows, HALF)], *columns, in2b, q3)[0]

    arrived = onward(last_columns(HALF))
    kept = last_columns(0)
    return jnp.concatenate([kept, arrived], axis=1)


def solution(mesh):
    return jax.shard_map(
        shards,
        mesh=mesh,
        in_specs=(P("row", "blk"), P(None, "blk")),
        out_specs=P("row", "blk"),
        check_vma=False,
    )
```

```python
import functools

import jax
import jax.numpy as jnp
from jax import lax
from jax.experimental import pallas as pl
from jax.experimental.pallas import tpu as pltpu
from jax.sharding import PartitionSpec as P

STEPS = 4
ROUNDS = 8
N = 256
HALF = 128
TILES = 64
PERIOD = N - 1


def dot(left, right, over=(1, 0), precision=lax.Precision.HIGHEST):
    return lax.dot_general(
        left,
        right,
        (((over[0],), (over[1],)), ((), ())),
        precision=precision,
        preferred_element_type=jnp.float32,
    )


def halved(values):
    high = values.astype(jnp.bfloat16)
    return high, (values - high.astype(jnp.float32)).astype(jnp.bfloat16)


def cross_dot(left, right, over=(1, 0)):
    numbers = (((over[0],), (over[1],)), ((), ()))
    (a, b), (c, d) = halved(left), halved(right)
    passes = [lax.dot_general(x, y, numbers, preferred_element_type=jnp.float32) for x, y in ((a, d), (b, c), (a, c))]
    return passes[0] + passes[1] + passes[2]


def seats(position, round_index):
    upper = position + round_index
    upper = jnp.where(upper >= PERIOD, upper - PERIOD, upper)
    lower = round_index - (position - HALF)
    lower = jnp.where(lower < 0, lower + PERIOD, lower)
    return jnp.where(position < HALF, upper, jnp.where(position == HALF, PERIOD, lower))


def placing(round_index, swapped=None):
    index = lax.broadcasted_iota(jnp.int32, (N, N), 0)
    if swapped is not None:
        index = jnp.where(swapped, jnp.where(index < HALF, index + HALF, index - HALF), index)
    position = lax.broadcasted_iota(jnp.int32, (N, N), 1)
    return (index == seats(position, round_index)).astype(jnp.bfloat16)


def thirds(values):
    high = values.astype(jnp.bfloat16)
    rest = values - high.astype(jnp.float32)
    middle = rest.astype(jnp.bfloat16)
    return high, middle, (rest - middle.astype(jnp.float32)).astype(jnp.bfloat16)


def placed(pieces, place, over):
    numbers = (((1,), (over,)), ((), ()))
    return [lax.dot_general(x, place, numbers, preferred_element_type=jnp.float32) for x in pieces]


def laid_both(values, place, over):
    columns = [x.astype(jnp.bfloat16) for x in placed(thirds(values), place, over)]
    numbers = (((over,), (0,)), ((), ()))
    return sum(lax.dot_general(place, x, numbers, preferred_element_type=jnp.float32) for x in columns)


def rotations(upper_diag, coupling, lower_diag, round_index):
    position = lax.broadcasted_iota(jnp.int32, (1, HALF), 1)
    is_lower = seats(position, round_index) < seats(position + HALF, round_index)
    difference = jnp.where(is_lower, lower_diag - upper_diag, upper_diag - lower_diag)
    x = jnp.abs(difference)
    y = jnp.where(difference >= 0.0, 2.0 * coupling, -2.0 * coupling)
    largest = jnp.maximum(x, jnp.abs(y))
    scale = jnp.where(largest > 0.0, largest, 1.0)
    inverse = 1.0 / scale
    x = jnp.where(largest > 0.0, x * inverse, 1.0)
    y = y * inverse
    tangent = y / (x + jnp.sqrt(x * x + y * y))
    cosine = 1.0 / jnp.sqrt(1.0 + tangent * tangent)
    sine = tangent * cosine
    return cosine, jnp.where(is_lower, -sine, sine)


def turn(upper, lower, cosine, sine):
    return cosine * upper + sine * lower, cosine * lower - sine * upper


def shift(upper, lower, axis):
    at = lax.broadcasted_iota(jnp.int32, upper.shape, axis)
    new_upper = jnp.where(at == HALF - 1, lower, pltpu.roll(upper, HALF - 1, axis))
    moved = pltpu.roll(jnp.where(at == 0, upper, lower), 1, axis)
    return new_upper, jnp.where(at == 0, lower, moved)


def jacobi(gram, offset, second, parts):
    uu, ul, lu, ll, qu, ql = parts
    start = placing(offset)
    laid_out = laid_both(gram, start, 0)
    uu[...] = laid_out[:HALF, :HALF]
    ul[...] = laid_out[:HALF, HALF:]
    lu[...] = laid_out[HALF:, :HALF]
    ll[...] = laid_out[HALF:, HALF:]
    qu[...] = start[:, :HALF].astype(jnp.float32)
    ql[...] = start[:, HALF:].astype(jnp.float32)
    shape = (HALF, HALF)
    eye = lax.broadcasted_iota(jnp.int32, shape, 0) == lax.broadcasted_iota(jnp.int32, shape, 1)

    def diagonal(ref):
        return jnp.sum(jnp.where(eye, ref[...], 0.0), axis=0, keepdims=True)

    def stood(row):
        return jnp.sum(jnp.where(eye, jnp.broadcast_to(row, shape), 0.0), axis=1, keepdims=True)

    for round_index in range(offset, offset + ROUNDS):
        cosine, sine = rotations(diagonal(uu), diagonal(ul), diagonal(ll), round_index)
        cosine_col, sine_col = stood(cosine), stood(sine)
        a, c = turn(uu[...], lu[...], cosine_col, sine_col)
        b, d = turn(ul[...], ll[...], cosine_col, sine_col)
        a, b = shift(*turn(a, b, cosine, sine), 1)
        c, d = shift(*turn(c, d, cosine, sine), 1)
        uu[...], lu[...] = shift(a, c, 0)
        ul[...], ll[...] = shift(b, d, 0)
        qu[...], ql[...] = shift(*turn(qu[...], ql[...], cosine, sine), 1)
    end = placing(offset + ROUNDS, second == 0)
    rotation = sum(placed(thirds(jnp.concatenate([qu[...], ql[...]], axis=1)), end, 1))
    upper = jnp.concatenate([uu[...], ul[...]], axis=1)
    lower = jnp.concatenate([lu[...], ll[...]], axis=1)
    rotated_gram = laid_both(jnp.concatenate([upper, lower], axis=0), end, 1)
    return rotation, rotated_gram


def joined(kept_gram, cross, moved_gram):
    upper = jnp.concatenate([kept_gram, cross], axis=1)
    lower = jnp.concatenate([cross.T, moved_gram], axis=1)
    return jnp.concatenate([upper, lower], axis=0)


def tiles(square):
    sides = [square[:, :HALF].reshape(-1, 1, 8, HALF), square[:, HALF:].reshape(-1, 1, 8, HALF)]
    return jnp.concatenate(sides, axis=1)


def square_of(received, place):
    count, height = received.shape[0], TILES // received.shape[0] * 8
    part = received[:, place * height : (place + 1) * height, :].reshape(TILES // 2, 2, 8, HALF)
    return jnp.concatenate([part[:, 0].reshape(N, HALF), part[:, 1].reshape(N, HALF)], axis=1)


def pack_kernel(skipped, received, *refs):
    *blocks, out = refs
    count, height = out.shape[0], TILES // out.shape[0] * 8
    if received is not None:
        spread = received.shape[1] - skipped * height
        own = jnp.sum(received[:, skipped * height :, :], axis=0, keepdims=True)
        out[:, :spread, :] = jnp.broadcast_to(own, (count, spread, HALF))
    else:
        spread = 0
    for number, block in enumerate(blocks):
        at = spread + number * height
        out[:, at : at + height, :] = tiles(block[...]).reshape(count, height, HALF)


def step0_kernel(second, received, out, h0, *parts):
    q0, rotated_gram = jacobi(square_of(received, 0), 0, second[0, 0], parts)
    h0[...] = rotated_gram[:HALF, :HALF]
    out[:N] = q0
    out[N:] = rotated_gram[HALF:]


def step1_kernel(second, received, h0, out0, in0, out, carried, *parts):
    q0_p = in0[:N]
    r1 = cross_dot(cross_dot(out0[:N], square_of(received, 1), (0, 0)), q0_p)
    out[N + HALF : 2 * N] = r1[HALF:]
    out[2 * N :] = q0_p
    carried[:, HALF:] = r1[:HALF, :HALF]
    q1, h1 = jacobi(joined(h0[...], r1[:HALF, HALF:], in0[N:, HALF:]), ROUNDS, second[1, 0], parts)
    out[:N] = q1
    out[N : N + HALF] = h1[HALF:]
    carried[:, :HALF] = h1[:HALF, :HALF]


def cross2_kernel(received, out0, in0, out1, in1, carried, out, kept, gram):
    q0_pp = in1[2 * N :]
    r2 = cross_dot(cross_dot(out0[:N], square_of(received, 0), (0, 0)), q0_pp)
    upper = jnp.concatenate([carried[:, HALF:], r2[:HALF, HALF:]], axis=1)
    lower = jnp.concatenate([in0[N:, :HALF], in1[N + HALF : 2 * N, HALF:]], axis=1)
    s1 = cross_dot(cross_dot(out1[:N], jnp.concatenate([upper, lower], axis=0), (0, 0)), in1[:N])
    gram[...] = joined(carried[:, :HALF], s1[:HALF, HALF:], in1[N : N + HALF, HALF:])
    out[:HALF] = s1[HALF:, HALF:]
    out[HALF:N] = r2[HALF:, HALF:]
    out[N : 2 * N] = in1[:N, HALF:]
    out[2 * N :] = q0_pp[:, HALF:]
    kept[:HALF] = s1[:HALF, :HALF]
    kept[HALF:] = r2[:HALF, :HALF]


def step2_kernel(second, gram, out, own, *parts):
    q2, h2 = jacobi(gram[...], 2 * ROUNDS, second[2, 0], parts)
    out[:N] = q2[:, HALF:]
    out[N:] = h2[HALF:, HALF:]
    own[:N] = q2[:, :HALF]
    own[N:] = h2[:HALF, :HALF]


def in_chunks(count, some_rows):
    step = min(N, count)

    def one(number, carry):
        some_rows(pl.ds(pl.multiple_of(number * step, step), step))
        return carry

    lax.fori_loop(0, count // step, one, 0)


def shadow_kernel(out0, in0, out1, in1, in2a, kept, own2, x0, x1, x2, x3, *refs):
    left_of_cross, ends, kept_cols, left_cols, right_cols, weights = refs
    q0_k, q1_k, q2_k, q0_pp = out0[:N, :HALF], out1[:N, :HALF], own2[:N], in1[2 * N :]
    q1_pp, q0_ppp = in2a[N : 2 * N], in2a[2 * N :]
    upper = jnp.concatenate([kept[HALF:], jnp.zeros((HALF, HALF), jnp.float32)], axis=1)
    lower = jnp.concatenate([in1[N + HALF : 2 * N, :HALF], in2a[HALF:N]], axis=1)
    t = cross_dot(q1_k, cross_dot(jnp.concatenate([upper, lower], axis=0), q1_pp), (0, 0))
    upper = jnp.concatenate([kept[:HALF], t], axis=1)
    lower = jnp.concatenate([in1[N : N + HALF, :HALF], in2a[:HALF]], axis=1)
    left_of_cross[...] = cross_dot(q2_k, jnp.concatenate([upper, lower], axis=0), (0, 0))

    q2_kk, q2_mk = own2[:HALF], own2[HALF:N]
    p1_kk, p1_mk, p1_km, p1_mm = in1[:HALF, :HALF], in1[HALF:N, :HALF], in1[:HALF, HALF:], in1[HALF:N, HALF:]
    weights[:, :HALF] = cross_dot(q0_k, cross_dot(out1[:HALF, :HALF], q2_kk))
    travelled = cross_dot(in0[:N, HALF:], cross_dot(out1[HALF:N, :HALF], q2_kk))
    weights[:, HALF:N] = travelled + cross_dot(in0[:N, :HALF], cross_dot(p1_km, q2_mk))
    weights[:, N : N + HALF] = cross_dot(in0[:N, :HALF], p1_kk)
    weights[:, N + HALF : 2 * N] = cross_dot(q0_pp[:, HALF:], cross_dot(p1_mm, q2_mk))
    weights[:, 2 * N : 2 * N + HALF] = cross_dot(q0_pp[:, HALF:], p1_mk)
    weights[:, 2 * N + HALF : 3 * N] = cross_dot(q0_pp[:, :HALF], q1_pp[:HALF])
    weights[:, 3 * N :] = cross_dot(q0_ppp, q1_pp[HALF:])
    ends[:, :HALF] = weights[:, :HALF]
    ends[:, HALF:] = weights[:, 3 * N :]

    def some_rows(rows):
        both = cross_dot(x1[rows, :], weights[:, HALF : N + HALF])
        three = cross_dot(x2[rows, :], weights[:, N + HALF : 3 * N])
        kept_cols[rows, :] = cross_dot(x0[rows, :], weights[:, :HALF]) + both[:, :HALF] + three[:, :HALF]
        left_cols[rows, :] = both[:, HALF:] + three[:, HALF:N]
        right_cols[rows, :] = three[:, N:] + cross_dot(x3[rows, :], weights[:, 3 * N :])

    in_chunks(kept_cols.shape[0], some_rows)


def last_kernel(place, kept_cols, left_cols, right_cols, in2b, q3, out):
    kept_weight, weight = q3[:HALF, place : place + HALF], q3[HALF:, place : place + HALF]
    left_weight, right_weight = cross_dot(in2b[:HALF], weight), cross_dot(in2b[HALF:N], weight)
    both = jnp.concatenate([kept_cols[...], left_cols[...]], axis=1)
    total = cross_dot(both, jnp.concatenate([kept_weight, left_weight], axis=0))
    out[...] = total + cross_dot(right_cols[...], right_weight)


def step3_kernel(second, received, left_of_cross, ends, own2, in2b, q3, *parts):
    farthest = cross_dot(square_of(received, 0), cross_dot(ends[:, HALF:], in2b[HALF:N]))
    cross = cross_dot(left_of_cross[...], in2b[:N]) + cross_dot(ends[:, :HALF], farthest, (0, 0))
    gram = joined(own2[N:], cross, in2b[N:])
    q3[...], _ = jacobi(gram, 3 * ROUNDS, second[3, 0], parts)


def products_kernel(left, right, out):
    out[...] = jnp.zeros(out.shape, jnp.float32)

    def some_rows(rows):
        out[...] += cross_dot(left[rows, :], right[rows, :], (0, 0))

    in_chunks(left.shape[0], some_rows)


JACOBI_PARTS = [pltpu.VMEM((HALF, HALF), jnp.float32)] * 4 + [pltpu.VMEM((N, HALF), jnp.float32)] * 2


def run(kernel, shapes, *operands, last=(), scratch=()):
    whole, smem = pl.BlockSpec(memory_space=pltpu.VMEM), pl.BlockSpec(memory_space=pltpu.SMEM)
    specs = [smem if x.dtype == jnp.int32 else whole for x in operands]
    specs += [pl.BlockSpec(memory_space=pl.ANY)] * len(last)

    def body(*refs):
        kernel(*refs[: len(operands)], *refs[len(operands) + len(last) :])

    return pl.pallas_call(
        body,
        out_shape=[jax.ShapeDtypeStruct(shape, jnp.float32) for shape in shapes],
        in_specs=specs,
        out_specs=[whole] * len(shapes),
        scratch_shapes=scratch,
        compiler_params=pltpu.CompilerParams(vmem_limit_bytes=16 * 2**20),
        cost_estimate=pl.CostEstimate(flops=10**6, bytes_accessed=2**10, transcendentals=0),
    )(*operands, *last)


def shards(matrix, sender_slot):
    devices, count = lax.axis_size("blk"), lax.axis_size("row")

    def onward(values, places=1):
        return lax.ppermute(values, "blk", [((i - places) % devices, i) for i in range(devices)])

    def products(other):
        return run(products_kernel, [(N, N)], matrix, other)[0]

    def exchange(received, skipped, *blocks, last=()):
        height = TILES // count * 8
        given = [] if received is None else [received]
        total = len(blocks) * height + (0 if received is None else received.shape[1] - skipped * height)

        def kernel(*refs):
            pack_kernel(skipped, refs[0] if given else None, *refs[len(given) :])

        (pieces,) = run(kernel, [(count, total, HALF)], *given, *blocks, last=last)
        return lax.all_to_all(pieces, "row", 0, 0, tiled=True)

    square, block = (N, N), (HALF, HALF)
    before1, gram = lax.optimization_barrier((onward(matrix), products(matrix)))
    received = exchange(None, 0, gram, products(before1))
    before2 = onward(before1)
    with_c1 = exchange(received, 0, products(before2))
    before3 = onward(before2)
    parts3 = products(before3)
    with_c2 = exchange(with_c1, 2, parts3)
    out0, h0 = run(
        step0_kernel, [(N + HALF, N), block], sender_slot, with_c1, scratch=JACOBI_PARTS, last=(parts3,)
    )
    in0 = onward(out0)
    out1, carried = run(
        step1_kernel,
        [(3 * N, N), (HALF, N)],
        *(sender_slot, with_c1, h0, out0, in0),
        scratch=JACOBI_PARTS,
    )
    in1 = onward(out1)
    with_c3 = exchange(with_c2, 1, last=(out1,))
    out2a, kept, gram2 = run(
        cross2_kernel,
        [(3 * N, HALF), (N, HALF), square],
        *(with_c2, out0, in0, out1, in1, carried),
    )
    in2a = onward(out2a)
    out2b, own2 = run(step2_kernel, [(N + HALF, HALF)] * 2, sender_slot, gram2, scratch=JACOBI_PARTS)
    in2b = onward(out2b)
    rows = matrix.shape[0]
    left_of_cross, ends, *columns = run(
        shadow_kernel,
        [(HALF, N), square] + [(rows, HALF)] * 3,
        *(out0, in0, out1, in1, in2a, kept, own2, matrix, before1, before2, before3),
        scratch=[pltpu.VMEM((N, 3 * N + HALF), jnp.float32)],
    )
    (q3,) = run(
        step3_kernel, [square], *(sender_slot, with_c3, left_of_cross, ends, own2, in2b), scratch=JACOBI_PARTS
    )

    def last_columns(place):
        return run(functools.partial(last_kernel, place), [(rows, HALF)], *columns, in2b, q3)[0]

    arrived = onward(last_columns(HALF))
    kept = last_columns(0)
    return jnp.concatenate([kept, arrived], axis=1)


def solution(mesh):
    return jax.shard_map(
        shards,
        mesh=mesh,
        in_specs=(P("row", "blk"), P(None, "blk")),
        out_specs=P("row", "blk"),
        check_vma=False,
    )
```

```python
import functools

import jax
import jax.numpy as jnp
from jax import lax
from jax.experimental import pallas as pl
from jax.experimental.pallas import tpu as pltpu
from jax.sharding import PartitionSpec as P

STEPS = 4
ROUNDS = 8
N = 256
HALF = 128
TILES = 64
PERIOD = N - 1


def dot(left, right, over=(1, 0), precision=lax.Precision.HIGHEST):
    return lax.dot_general(
        left,
        right,
        (((over[0],), (over[1],)), ((), ())),
        precision=precision,
        preferred_element_type=jnp.float32,
    )


def halved(values):
    high = values.astype(jnp.bfloat16)
    return high, (values - high.astype(jnp.float32)).astype(jnp.bfloat16)


def cross_dot(left, right, over=(1, 0)):
    numbers = (((over[0],), (over[1],)), ((), ()))
    (a, b), (c, d) = halved(left), halved(right)
    passes = [lax.dot_general(x, y, numbers, preferred_element_type=jnp.float32) for x, y in ((a, d), (b, c), (a, c))]
    return passes[0] + passes[1] + passes[2]


def seats(position, round_index):
    upper = position + round_index
    upper = jnp.where(upper >= PERIOD, upper - PERIOD, upper)
    lower = round_index - (position - HALF)
    lower = jnp.where(lower < 0, lower + PERIOD, lower)
    return jnp.where(position < HALF, upper, jnp.where(position == HALF, PERIOD, lower))


def placing(round_index, swapped=None):
    index = lax.broadcasted_iota(jnp.int32, (N, N), 0)
    if swapped is not None:
        index = jnp.where(swapped, jnp.where(index < HALF, index + HALF, index - HALF), index)
    position = lax.broadcasted_iota(jnp.int32, (N, N), 1)
    return (index == seats(position, round_index)).astype(jnp.bfloat16)


def thirds(values):
    high = values.astype(jnp.bfloat16)
    rest = values - high.astype(jnp.float32)
    middle = rest.astype(jnp.bfloat16)
    return high, middle, (rest - middle.astype(jnp.float32)).astype(jnp.bfloat16)


def placed(pieces, place, over):
    numbers = (((1,), (over,)), ((), ()))
    return [lax.dot_general(x, place, numbers, preferred_element_type=jnp.float32) for x in pieces]


def laid_both(values, place, over):
    columns = [x.astype(jnp.bfloat16) for x in placed(thirds(values), place, over)]
    numbers = (((over,), (0,)), ((), ()))
    return sum(lax.dot_general(place, x, numbers, preferred_element_type=jnp.float32) for x in columns)


def rotations(upper_diag, coupling, lower_diag, round_index):
    position = lax.broadcasted_iota(jnp.int32, (1, HALF), 1)
    is_lower = seats(position, round_index) < seats(position + HALF, round_index)
    difference = jnp.where(is_lower, lower_diag - upper_diag, upper_diag - lower_diag)
    x = jnp.abs(difference)
    y = jnp.where(difference >= 0.0, 2.0 * coupling, -2.0 * coupling)
    largest = jnp.maximum(x, jnp.abs(y))
    scale = jnp.where(largest > 0.0, largest, 1.0)
    inverse = 1.0 / scale
    x = jnp.where(largest > 0.0, x * inverse, 1.0)
    y = y * inverse
    tangent = y / (x + jnp.sqrt(x * x + y * y))
    cosine = 1.0 / jnp.sqrt(1.0 + tangent * tangent)
    sine = tangent * cosine
    return cosine, jnp.where(is_lower, -sine, sine)


def turn(upper, lower, cosine, sine):
    return cosine * upper + sine * lower, cosine * lower - sine * upper


def shift(upper, lower, axis):
    at = lax.broadcasted_iota(jnp.int32, upper.shape, axis)
    new_upper = jnp.where(at == HALF - 1, lower, pltpu.roll(upper, HALF - 1, axis))
    moved = pltpu.roll(jnp.where(at == 0, upper, lower), 1, axis)
    return new_upper, jnp.where(at == 0, lower, moved)


def jacobi(gram, offset, second, parts):
    uu, ul, lu, ll, qu, ql = parts
    start = placing(offset)
    laid_out = laid_both(gram, start, 0)
    uu[...] = laid_out[:HALF, :HALF]
    ul[...] = laid_out[:HALF, HALF:]
    lu[...] = laid_out[HALF:, :HALF]
    ll[...] = laid_out[HALF:, HALF:]
    qu[...] = start[:, :HALF].astype(jnp.float32)
    ql[...] = start[:, HALF:].astype(jnp.float32)
    shape = (HALF, HALF)
    eye = lax.broadcasted_iota(jnp.int32, shape, 0) == lax.broadcasted_iota(jnp.int32, shape, 1)

    def diagonal(ref):
        return jnp.sum(jnp.where(eye, ref[...], 0.0), axis=0, keepdims=True)

    def stood(row):
        return jnp.sum(jnp.where(eye, jnp.broadcast_to(row, shape), 0.0), axis=1, keepdims=True)

    for round_index in range(offset, offset + ROUNDS):
        cosine, sine = rotations(diagonal(uu), diagonal(ul), diagonal(ll), round_index)
        cosine_col, sine_col = stood(cosine), stood(sine)
        a, c = turn(uu[...], lu[...], cosine_col, sine_col)
        b, d = turn(ul[...], ll[...], cosine_col, sine_col)
        a, b = shift(*turn(a, b, cosine, sine), 1)
        c, d = shift(*turn(c, d, cosine, sine), 1)
        uu[...], lu[...] = shift(a, c, 0)
        ul[...], ll[...] = shift(b, d, 0)
        qu[...], ql[...] = shift(*turn(qu[...], ql[...], cosine, sine), 1)
    end = placing(offset + ROUNDS, second == 0)
    rotation = sum(placed(thirds(jnp.concatenate([qu[...], ql[...]], axis=1)), end, 1))
    upper = jnp.concatenate([uu[...], ul[...]], axis=1)
    lower = jnp.concatenate([lu[...], ll[...]], axis=1)
    rotated_gram = laid_both(jnp.concatenate([upper, lower], axis=0), end, 1)
    return rotation, rotated_gram


def joined(kept_gram, cross, moved_gram):
    upper = jnp.concatenate([kept_gram, cross], axis=1)
    lower = jnp.concatenate([cross.T, moved_gram], axis=1)
    return jnp.concatenate([upper, lower], axis=0)


def tiles(square):
    sides = [square[:, :HALF].reshape(-1, 1, 8, HALF), square[:, HALF:].reshape(-1, 1, 8, HALF)]
    return jnp.concatenate(sides, axis=1)


def square_of(received, place):
    count, height = received.shape[0], TILES // received.shape[0] * 8
    part = received[:, place * height : (place + 1) * height, :].reshape(TILES // 2, 2, 8, HALF)
    return jnp.concatenate([part[:, 0].reshape(N, HALF), part[:, 1].reshape(N, HALF)], axis=1)


def pack_kernel(skipped, received, *refs):
    *blocks, out = refs
    count, height = out.shape[0], TILES // out.shape[0] * 8
    if received is not None:
        spread = received.shape[1] - skipped * height
        own = jnp.sum(received[:, skipped * height :, :], axis=0, keepdims=True)
        out[:, :spread, :] = jnp.broadcast_to(own, (count, spread, HALF))
    else:
        spread = 0
    for number, block in enumerate(blocks):
        at = spread + number * height
        out[:, at : at + height, :] = tiles(block[...]).reshape(count, height, HALF)


def step0_kernel(second, received, out, h0, *parts):
    q0, rotated_gram = jacobi(square_of(received, 0), 0, second[0, 0], parts)
    h0[...] = rotated_gram[:HALF, :HALF]
    out[:N] = q0
    out[N:] = rotated_gram[HALF:]


def step1_kernel(second, received, h0, out0, in0, out, carried, *parts):
    q0_p = in0[:N]
    r1 = cross_dot(cross_dot(out0[:N], square_of(received, 1), (0, 0)), q0_p)
    out[N + HALF : 2 * N] = r1[HALF:]
    out[2 * N :] = q0_p
    carried[:, HALF:] = r1[:HALF, :HALF]
    q1, h1 = jacobi(joined(h0[...], r1[:HALF, HALF:], in0[N:, HALF:]), ROUNDS, second[1, 0], parts)
    out[:N] = q1
    out[N : N + HALF] = h1[HALF:]
    carried[:, :HALF] = h1[:HALF, :HALF]


def cross2_kernel(received, out0, in0, out1, in1, carried, out, kept, gram):
    q0_pp = in1[2 * N :]
    r2 = cross_dot(cross_dot(out0[:N], square_of(received, 0), (0, 0)), q0_pp)
    upper = jnp.concatenate([carried[:, HALF:], r2[:HALF, HALF:]], axis=1)
    lower = jnp.concatenate([in0[N:, :HALF], in1[N + HALF : 2 * N, HALF:]], axis=1)
    s1 = cross_dot(cross_dot(out1[:N], jnp.concatenate([upper, lower], axis=0), (0, 0)), in1[:N])
    gram[...] = joined(carried[:, :HALF], s1[:HALF, HALF:], in1[N : N + HALF, HALF:])
    out[:HALF] = s1[HALF:, HALF:]
    out[HALF:N] = r2[HALF:, HALF:]
    out[N : 2 * N] = in1[:N, HALF:]
    out[2 * N :] = q0_pp[:, HALF:]
    kept[:HALF] = s1[:HALF, :HALF]
    kept[HALF:] = r2[:HALF, :HALF]


def step2_kernel(second, gram, out, own, *parts):
    q2, h2 = jacobi(gram[...], 2 * ROUNDS, second[2, 0], parts)
    out[:N] = q2[:, HALF:]
    out[N:] = h2[HALF:, HALF:]
    own[:N] = q2[:, :HALF]
    own[N:] = h2[:HALF, :HALF]


def in_chunks(count, some_rows):
    step = min(N, count)

    def one(number, carry):
        some_rows(pl.ds(pl.multiple_of(number * step, step), step))
        return carry

    lax.fori_loop(0, count // step, one, 0)


def columns_kernel(out0, in0, out1, in1, own2, x0, x1, x2, pair, end, weights):
    q2_kk, q2_mk, q0_pp = own2[:HALF], own2[HALF:N], in1[2 * N :]
    p1_kk, p1_mk, p1_km, p1_mm = in1[:HALF, :HALF], in1[HALF:N, :HALF], in1[:HALF, HALF:], in1[HALF:N, HALF:]
    end[...] = cross_dot(out0[:N, :HALF], cross_dot(out1[:HALF, :HALF], q2_kk))
    travelled = cross_dot(in0[:N, HALF:], cross_dot(out1[HALF:N, :HALF], q2_kk))
    weights[:, :HALF] = travelled + cross_dot(in0[:N, :HALF], cross_dot(p1_km, q2_mk))
    weights[:, HALF:N] = cross_dot(in0[:N, :HALF], p1_kk)
    weights[:, N : N + HALF] = cross_dot(q0_pp[:, HALF:], cross_dot(p1_mm, q2_mk))
    weights[:, N + HALF :] = cross_dot(q0_pp[:, HALF:], p1_mk)

    def some_rows(rows):
        both = cross_dot(x1[rows, :], weights[:, :N]) + cross_dot(x2[rows, :], weights[:, N:])
        pair[rows, :HALF] = cross_dot(x0[rows, :], end[...]) + both[:, :HALF]
        pair[rows, HALF:] = both[:, HALF:]

    in_chunks(pair.shape[0], some_rows)


def cross3_kernel(out0, out1, in1, in2a, kept, own2, end, x2, x3, ends, right_cols, weights):
    q1_k, q2_k = out1[:N, :HALF], own2[:N]
    q1_pp, q0_ppp = in2a[N : 2 * N], in2a[2 * N :]
    upper = jnp.concatenate([kept[HALF:], jnp.zeros((HALF, HALF), jnp.float32)], axis=1)
    lower = jnp.concatenate([in1[N + HALF : 2 * N, :HALF], in2a[HALF:N]], axis=1)
    t = cross_dot(q1_k, cross_dot(jnp.concatenate([upper, lower], axis=0), q1_pp), (0, 0))
    upper = jnp.concatenate([kept[:HALF], t], axis=1)
    lower = jnp.concatenate([in1[N : N + HALF, :HALF], in2a[:HALF]], axis=1)
    ends[N:] = cross_dot(q2_k, jnp.concatenate([upper, lower], axis=0), (0, 0))
    weights[:, :HALF] = cross_dot(in1[2 * N :, :HALF], q1_pp[:HALF])
    weights[:, HALF:] = cross_dot(q0_ppp, q1_pp[HALF:])
    ends[:N, :HALF] = end[...]
    ends[:N, HALF:] = weights[:, HALF:]

    def some_rows(rows):
        right_cols[rows, :] = cross_dot(x2[rows, :], weights[:, :HALF]) + cross_dot(x3[rows, :], weights[:, HALF:])

    in_chunks(right_cols.shape[0], some_rows)


def last_kernel(place, pair, right_cols, in2b, q3, out):
    kept_weight, weight = q3[:HALF, place : place + HALF], q3[HALF:, place : place + HALF]
    left_weight, right_weight = cross_dot(in2b[:HALF], weight), cross_dot(in2b[HALF:N], weight)
    total = cross_dot(pair[...], jnp.concatenate([kept_weight, left_weight], axis=0))
    out[...] = total + cross_dot(right_cols[...], right_weight)


def step3_kernel(second, received, ends, own2, in2b, q3, *parts):
    farthest = cross_dot(square_of(received, 0), cross_dot(ends[:N, HALF:], in2b[HALF:N]))
    cross = cross_dot(ends[N:], in2b[:N]) + cross_dot(ends[:N, :HALF], farthest, (0, 0))
    gram = joined(own2[N:], cross, in2b[N:])
    q3[...], _ = jacobi(gram, 3 * ROUNDS, second[3, 0], parts)


def products_kernel(left, right, out):
    out[...] = jnp.zeros(out.shape, jnp.float32)

    def some_rows(rows):
        out[...] += cross_dot(left[rows, :], right[rows, :], (0, 0))

    in_chunks(left.shape[0], some_rows)


JACOBI_PARTS = [pltpu.VMEM((HALF, HALF), jnp.float32)] * 4 + [pltpu.VMEM((N, HALF), jnp.float32)] * 2


def run(kernel, shapes, *operands, last=(), scratch=()):
    whole, smem = pl.BlockSpec(memory_space=pltpu.VMEM), pl.BlockSpec(memory_space=pltpu.SMEM)
    specs = [smem if x.dtype == jnp.int32 else whole for x in operands]
    specs += [pl.BlockSpec(memory_space=pl.ANY)] * len(last)

    def body(*refs):
        kernel(*refs[: len(operands)], *refs[len(operands) + len(last) :])

    return pl.pallas_call(
        body,
        out_shape=[jax.ShapeDtypeStruct(shape, jnp.float32) for shape in shapes],
        in_specs=specs,
        out_specs=[whole] * len(shapes),
        scratch_shapes=scratch,
        compiler_params=pltpu.CompilerParams(vmem_limit_bytes=16 * 2**20),
        cost_estimate=pl.CostEstimate(flops=10**6, bytes_accessed=2**10, transcendentals=0),
    )(*operands, *last)


def shards(matrix, sender_slot):
    devices, count = lax.axis_size("blk"), lax.axis_size("row")

    def onward(values, places=1):
        return lax.ppermute(values, "blk", [((i - places) % devices, i) for i in range(devices)])

    def products(other):
        return run(products_kernel, [(N, N)], matrix, other)[0]

    def exchange(received, skipped, *blocks, last=()):
        height = TILES // count * 8
        given = [] if received is None else [received]
        total = len(blocks) * height + (0 if received is None else received.shape[1] - skipped * height)

        def kernel(*refs):
            pack_kernel(skipped, refs[0] if given else None, *refs[len(given) :])

        (pieces,) = run(kernel, [(count, total, HALF)], *given, *blocks, last=last)
        return lax.all_to_all(pieces, "row", 0, 0, tiled=True)

    square, block = (N, N), (HALF, HALF)
    before1, gram = lax.optimization_barrier((onward(matrix), products(matrix)))
    received = exchange(None, 0, gram, products(before1))
    before2 = onward(before1)
    with_c1 = exchange(received, 0, products(before2))
    before3 = onward(before2)
    parts3 = products(before3)
    with_c2 = exchange(with_c1, 2, parts3)
    out0, h0 = run(
        step0_kernel, [(N + HALF, N), block], sender_slot, with_c1, scratch=JACOBI_PARTS, last=(parts3,)
    )
    in0 = onward(out0)
    out1, carried = run(
        step1_kernel,
        [(3 * N, N), (HALF, N)],
        *(sender_slot, with_c1, h0, out0, in0),
        scratch=JACOBI_PARTS,
    )
    in1 = onward(out1)
    with_c3 = exchange(with_c2, 1, last=(out1,))
    out2a, kept, gram2 = run(
        cross2_kernel,
        [(3 * N, HALF), (N, HALF), square],
        *(with_c2, out0, in0, out1, in1, carried),
    )
    in2a = onward(out2a)
    out2b, own2 = run(step2_kernel, [(N + HALF, HALF)] * 2, sender_slot, gram2, scratch=JACOBI_PARTS)
    in2b = onward(out2b)
    rows = matrix.shape[0]
    pair, end = run(
        columns_kernel,
        [(rows, N), (N, HALF)],
        *(out0, in0, out1, in1, own2, matrix, before1, before2),
        scratch=[pltpu.VMEM((N, 2 * N), jnp.float32)],
    )
    ends, right_cols = run(
        cross3_kernel,
        [(N + HALF, N), (rows, HALF)],
        *(out0, out1, in1, in2a, kept, own2, end, before2, before3),
        scratch=[pltpu.VMEM((N, N), jnp.float32)],
    )
    (q3,) = run(step3_kernel, [square], *(sender_slot, with_c3, ends, own2, in2b), scratch=JACOBI_PARTS)

    def last_columns(place):
        return run(functools.partial(last_kernel, place), [(rows, HALF)], pair, right_cols, in2b, q3)[0]

    arrived = onward(last_columns(HALF))
    kept = last_columns(0)
    return jnp.concatenate([kept, arrived], axis=1)


def solution(mesh):
    return jax.shard_map(
        shards,
        mesh=mesh,
        in_specs=(P("row", "blk"), P(None, "blk")),
        out_specs=P("row", "blk"),
        check_vma=False,
    )
```

```python
import functools

import jax
import jax.numpy as jnp
from jax import lax
from jax.experimental import pallas as pl
from jax.experimental.pallas import tpu as pltpu
from jax.sharding import PartitionSpec as P

STEPS = 4
ROUNDS = 8
N = 256
HALF = 128
TILES = 64
PERIOD = N - 1


def dot(left, right, over=(1, 0), precision=lax.Precision.HIGHEST):
    return lax.dot_general(
        left,
        right,
        (((over[0],), (over[1],)), ((), ())),
        precision=precision,
        preferred_element_type=jnp.float32,
    )


def halved(values):
    high = values.astype(jnp.bfloat16)
    return high, (values - high.astype(jnp.float32)).astype(jnp.bfloat16)


def cross_dot(left, right, over=(1, 0)):
    numbers = (((over[0],), (over[1],)), ((), ()))
    (a, b), (c, d) = halved(left), halved(right)
    passes = [lax.dot_general(x, y, numbers, preferred_element_type=jnp.float32) for x, y in ((a, d), (b, c), (a, c))]
    return passes[0] + passes[1] + passes[2]


def seats(position, round_index):
    upper = position + round_index
    upper = jnp.where(upper >= PERIOD, upper - PERIOD, upper)
    lower = round_index - (position - HALF)
    lower = jnp.where(lower < 0, lower + PERIOD, lower)
    return jnp.where(position < HALF, upper, jnp.where(position == HALF, PERIOD, lower))


def placing(round_index, swapped=None):
    index = lax.broadcasted_iota(jnp.int32, (N, N), 0)
    if swapped is not None:
        index = jnp.where(swapped, jnp.where(index < HALF, index + HALF, index - HALF), index)
    position = lax.broadcasted_iota(jnp.int32, (N, N), 1)
    return (index == seats(position, round_index)).astype(jnp.bfloat16)


def thirds(values):
    high = values.astype(jnp.bfloat16)
    rest = values - high.astype(jnp.float32)
    middle = rest.astype(jnp.bfloat16)
    return high, middle, (rest - middle.astype(jnp.float32)).astype(jnp.bfloat16)


def placed(pieces, place, over):
    numbers = (((1,), (over,)), ((), ()))
    return [lax.dot_general(x, place, numbers, preferred_element_type=jnp.float32) for x in pieces]


def laid_both(values, place, over):
    columns = [x.astype(jnp.bfloat16) for x in placed(thirds(values), place, over)]
    numbers = (((over,), (0,)), ((), ()))
    return sum(lax.dot_general(place, x, numbers, preferred_element_type=jnp.float32) for x in columns)


def rotations(upper_diag, coupling, lower_diag, round_index):
    position = lax.broadcasted_iota(jnp.int32, (1, HALF), 1)
    is_lower = seats(position, round_index) < seats(position + HALF, round_index)
    difference = jnp.where(is_lower, lower_diag - upper_diag, upper_diag - lower_diag)
    x = jnp.abs(difference)
    y = jnp.where(difference >= 0.0, 2.0 * coupling, -2.0 * coupling)
    largest = jnp.maximum(x, jnp.abs(y))
    scale = jnp.where(largest > 0.0, largest, 1.0)
    inverse = 1.0 / scale
    x = jnp.where(largest > 0.0, x * inverse, 1.0)
    y = y * inverse
    tangent = y / (x + jnp.sqrt(x * x + y * y))
    cosine = 1.0 / jnp.sqrt(1.0 + tangent * tangent)
    sine = tangent * cosine
    return cosine, jnp.where(is_lower, -sine, sine)


def turn(upper, lower, cosine, sine):
    return cosine * upper + sine * lower, cosine * lower - sine * upper


def shift(upper, lower, axis):
    at = lax.broadcasted_iota(jnp.int32, upper.shape, axis)
    new_upper = jnp.where(at == HALF - 1, lower, pltpu.roll(upper, HALF - 1, axis))
    moved = pltpu.roll(jnp.where(at == 0, upper, lower), 1, axis)
    return new_upper, jnp.where(at == 0, lower, moved)


def jacobi(gram, offset, second, parts):
    uu, ul, lu, ll, qu, ql = parts
    start = placing(offset)
    laid_out = laid_both(gram, start, 0)
    uu[...] = laid_out[:HALF, :HALF]
    ul[...] = laid_out[:HALF, HALF:]
    lu[...] = laid_out[HALF:, :HALF]
    ll[...] = laid_out[HALF:, HALF:]
    qu[...] = start[:, :HALF].astype(jnp.float32)
    ql[...] = start[:, HALF:].astype(jnp.float32)
    shape = (HALF, HALF)
    eye = lax.broadcasted_iota(jnp.int32, shape, 0) == lax.broadcasted_iota(jnp.int32, shape, 1)

    def diagonal(ref):
        return jnp.sum(jnp.where(eye, ref[...], 0.0), axis=0, keepdims=True)

    def stood(row):
        return jnp.sum(jnp.where(eye, jnp.broadcast_to(row, shape), 0.0), axis=1, keepdims=True)

    for round_index in range(offset, offset + ROUNDS):
        cosine, sine = rotations(diagonal(uu), diagonal(ul), diagonal(ll), round_index)
        cosine_col, sine_col = stood(cosine), stood(sine)
        a, c = turn(uu[...], lu[...], cosine_col, sine_col)
        b, d = turn(ul[...], ll[...], cosine_col, sine_col)
        a, b = shift(*turn(a, b, cosine, sine), 1)
        c, d = shift(*turn(c, d, cosine, sine), 1)
        uu[...], lu[...] = shift(a, c, 0)
        ul[...], ll[...] = shift(b, d, 0)
        qu[...], ql[...] = shift(*turn(qu[...], ql[...], cosine, sine), 1)
    end = placing(offset + ROUNDS, second == 0)
    rotation = sum(placed(thirds(jnp.concatenate([qu[...], ql[...]], axis=1)), end, 1))
    upper = jnp.concatenate([uu[...], ul[...]], axis=1)
    lower = jnp.concatenate([lu[...], ll[...]], axis=1)
    rotated_gram = laid_both(jnp.concatenate([upper, lower], axis=0), end, 1)
    return rotation, rotated_gram


def joined(kept_gram, cross, moved_gram):
    upper = jnp.concatenate([kept_gram, cross], axis=1)
    lower = jnp.concatenate([cross.T, moved_gram], axis=1)
    return jnp.concatenate([upper, lower], axis=0)


def tiles(square):
    sides = [square[:, :HALF].reshape(-1, 1, 8, HALF), square[:, HALF:].reshape(-1, 1, 8, HALF)]
    return jnp.concatenate(sides, axis=1)


def square_of(received, place):
    count, height = received.shape[0], TILES // received.shape[0] * 8
    part = received[:, place * height : (place + 1) * height, :].reshape(TILES // 2, 2, 8, HALF)
    return jnp.concatenate([part[:, 0].reshape(N, HALF), part[:, 1].reshape(N, HALF)], axis=1)


def pack_kernel(skipped, received, *refs):
    *blocks, out = refs
    count, height = out.shape[0], TILES // out.shape[0] * 8
    if received is not None:
        spread = received.shape[1] - skipped * height
        own = jnp.sum(received[:, skipped * height :, :], axis=0, keepdims=True)
        out[:, :spread, :] = jnp.broadcast_to(own, (count, spread, HALF))
    else:
        spread = 0
    for number, block in enumerate(blocks):
        at = spread + number * height
        out[:, at : at + height, :] = tiles(block[...]).reshape(count, height, HALF)


def step0_kernel(second, received, out, h0, *parts):
    q0, rotated_gram = jacobi(square_of(received, 0), 0, second[0, 0], parts)
    h0[...] = rotated_gram[:HALF, :HALF]
    out[:N] = q0
    out[N:] = rotated_gram[HALF:]


def step1_kernel(second, received, h0, out0, in0, out, carried, *parts):
    q0_p = in0[:N]
    r1 = cross_dot(cross_dot(out0[:N], square_of(received, 1), (0, 0)), q0_p)
    out[N + HALF : 2 * N] = r1[HALF:]
    out[2 * N :] = q0_p
    carried[:, HALF:] = r1[:HALF, :HALF]
    q1, h1 = jacobi(joined(h0[...], r1[:HALF, HALF:], in0[N:, HALF:]), ROUNDS, second[1, 0], parts)
    out[:N] = q1
    out[N : N + HALF] = h1[HALF:]
    carried[:, :HALF] = h1[:HALF, :HALF]


def cross2_kernel(received, out0, in0, out1, in1, carried, out, kept, gram):
    q0_pp = in1[2 * N :]
    r2 = cross_dot(cross_dot(out0[:N], square_of(received, 0), (0, 0)), q0_pp)
    upper = jnp.concatenate([carried[:, HALF:], r2[:HALF, HALF:]], axis=1)
    lower = jnp.concatenate([in0[N:, :HALF], in1[N + HALF : 2 * N, HALF:]], axis=1)
    s1 = cross_dot(cross_dot(out1[:N], jnp.concatenate([upper, lower], axis=0), (0, 0)), in1[:N])
    gram[...] = joined(carried[:, :HALF], s1[:HALF, HALF:], in1[N : N + HALF, HALF:])
    out[:HALF] = s1[HALF:, HALF:]
    out[HALF:N] = r2[HALF:, HALF:]
    out[N : 2 * N] = in1[:N, HALF:]
    out[2 * N :] = q0_pp[:, HALF:]
    kept[:HALF] = s1[:HALF, :HALF]
    kept[HALF:] = r2[:HALF, :HALF]


def step2_kernel(second, gram, out, own, *parts):
    q2, h2 = jacobi(gram[...], 2 * ROUNDS, second[2, 0], parts)
    out[:N] = q2[:, HALF:]
    out[N:] = h2[HALF:, HALF:]
    own[:N] = q2[:, :HALF]
    own[N:] = h2[:HALF, :HALF]


def in_chunks(count, some_rows):
    step = min(N, count)

    def one(number, carry):
        some_rows(pl.ds(pl.multiple_of(number * step, step), step))
        return carry

    lax.fori_loop(0, count // step, one, 0)


def columns_kernel(out0, in0, out1, in1, own2, x0, x1, x2, pair, end, weights):
    q2_kk, q2_mk, q0_pp = own2[:HALF], own2[HALF:N], in1[2 * N :]
    p1_kk, p1_mk, p1_km, p1_mm = in1[:HALF, :HALF], in1[HALF:N, :HALF], in1[:HALF, HALF:], in1[HALF:N, HALF:]
    end[...] = cross_dot(out0[:N, :HALF], cross_dot(out1[:HALF, :HALF], q2_kk))
    travelled = cross_dot(in0[:N, HALF:], cross_dot(out1[HALF:N, :HALF], q2_kk))
    weights[:, :HALF] = travelled + cross_dot(in0[:N, :HALF], cross_dot(p1_km, q2_mk))
    weights[:, HALF:N] = cross_dot(in0[:N, :HALF], p1_kk)
    weights[:, N : N + HALF] = cross_dot(q0_pp[:, HALF:], cross_dot(p1_mm, q2_mk))
    weights[:, N + HALF :] = cross_dot(q0_pp[:, HALF:], p1_mk)

    def some_rows(rows):
        both = cross_dot(x1[rows, :], weights[:, :N]) + cross_dot(x2[rows, :], weights[:, N:])
        pair[rows, :HALF] = cross_dot(x0[rows, :], end[...]) + both[:, :HALF]
        pair[rows, HALF:] = both[:, HALF:]

    in_chunks(pair.shape[0], some_rows)


def cross3_kernel(out0, out1, in1, in2a, kept, own2, end, x2, x3, ends, right_cols, weights):
    q1_k, q2_k = out1[:N, :HALF], own2[:N]
    q1_pp, q0_ppp = in2a[N : 2 * N], in2a[2 * N :]
    upper = jnp.concatenate([kept[HALF:], jnp.zeros((HALF, HALF), jnp.float32)], axis=1)
    lower = jnp.concatenate([in1[N + HALF : 2 * N, :HALF], in2a[HALF:N]], axis=1)
    t = cross_dot(q1_k, cross_dot(jnp.concatenate([upper, lower], axis=0), q1_pp), (0, 0))
    upper = jnp.concatenate([kept[:HALF], t], axis=1)
    lower = jnp.concatenate([in1[N : N + HALF, :HALF], in2a[:HALF]], axis=1)
    ends[N:] = cross_dot(q2_k, jnp.concatenate([upper, lower], axis=0), (0, 0))
    weights[:, :HALF] = cross_dot(in1[2 * N :, :HALF], q1_pp[:HALF])
    weights[:, HALF:] = cross_dot(q0_ppp, q1_pp[HALF:])
    ends[:N, :HALF] = end[...]
    ends[:N, HALF:] = weights[:, HALF:]

    def some_rows(rows):
        right_cols[rows, :] = cross_dot(x2[rows, :], weights[:, :HALF]) + cross_dot(x3[rows, :], weights[:, HALF:])

    in_chunks(right_cols.shape[0], some_rows)


def last_kernel(place, pair, right_cols, in2b, q3, out):
    kept_weight, weight = q3[:HALF, place : place + HALF], q3[HALF:, place : place + HALF]
    left_weight, right_weight = cross_dot(in2b[:HALF], weight), cross_dot(in2b[HALF:N], weight)
    total = cross_dot(pair[...], jnp.concatenate([kept_weight, left_weight], axis=0))
    out[...] = total + cross_dot(right_cols[...], right_weight)


def join_kernel(kept, arrived, out, sems):
    step, copies = kept.shape[0] // 4, []
    for number in range(4):
        rows = pl.ds(number * step, step)
        for side, half in enumerate((kept, arrived)):
            target = out.at[rows, pl.ds(side * HALF, HALF)]
            copies.append(pltpu.make_async_copy(half.at[rows, :], target, sems.at[2 * number + side]))
    for copy in copies:
        copy.start()
    for copy in copies:
        copy.wait()


def step3_kernel(second, received, ends, own2, in2b, q3, *parts):
    farthest = cross_dot(square_of(received, 0), cross_dot(ends[:N, HALF:], in2b[HALF:N]))
    cross = cross_dot(ends[N:], in2b[:N]) + cross_dot(ends[:N, :HALF], farthest, (0, 0))
    gram = joined(own2[N:], cross, in2b[N:])
    q3[...], _ = jacobi(gram, 3 * ROUNDS, second[3, 0], parts)


def products_kernel(left, right, out):
    out[...] = jnp.zeros(out.shape, jnp.float32)

    def some_rows(rows):
        out[...] += cross_dot(left[rows, :], right[rows, :], (0, 0))

    in_chunks(left.shape[0], some_rows)


JACOBI_PARTS = [pltpu.VMEM((HALF, HALF), jnp.float32)] * 4 + [pltpu.VMEM((N, HALF), jnp.float32)] * 2


def run(kernel, shapes, *operands, last=(), scratch=()):
    whole, smem = pl.BlockSpec(memory_space=pltpu.VMEM), pl.BlockSpec(memory_space=pltpu.SMEM)
    specs = [smem if x.dtype == jnp.int32 else whole for x in operands]
    specs += [pl.BlockSpec(memory_space=pl.ANY)] * len(last)

    def body(*refs):
        kernel(*refs[: len(operands)], *refs[len(operands) + len(last) :])

    return pl.pallas_call(
        body,
        out_shape=[jax.ShapeDtypeStruct(shape, jnp.float32) for shape in shapes],
        in_specs=specs,
        out_specs=[whole] * len(shapes),
        scratch_shapes=scratch,
        compiler_params=pltpu.CompilerParams(vmem_limit_bytes=16 * 2**20),
        cost_estimate=pl.CostEstimate(flops=10**6, bytes_accessed=2**10, transcendentals=0),
    )(*operands, *last)


def shards(matrix, sender_slot):
    devices, count = lax.axis_size("blk"), lax.axis_size("row")

    def onward(values, places=1):
        return lax.ppermute(values, "blk", [((i - places) % devices, i) for i in range(devices)])

    def products(other):
        return run(products_kernel, [(N, N)], matrix, other)[0]

    def exchange(received, skipped, *blocks, last=()):
        height = TILES // count * 8
        given = [] if received is None else [received]
        total = len(blocks) * height + (0 if received is None else received.shape[1] - skipped * height)

        def kernel(*refs):
            pack_kernel(skipped, refs[0] if given else None, *refs[len(given) :])

        (pieces,) = run(kernel, [(count, total, HALF)], *given, *blocks, last=last)
        return lax.all_to_all(pieces, "row", 0, 0, tiled=True)

    square, block = (N, N), (HALF, HALF)
    before1, gram = lax.optimization_barrier((onward(matrix), products(matrix)))
    received = exchange(None, 0, gram, products(before1))
    before2 = onward(before1)
    with_c1 = exchange(received, 0, products(before2))
    before3 = onward(before2)
    parts3 = products(before3)
    with_c2 = exchange(with_c1, 2, parts3)
    out0, h0 = run(
        step0_kernel, [(N + HALF, N), block], sender_slot, with_c1, scratch=JACOBI_PARTS, last=(parts3,)
    )
    in0 = onward(out0)
    out1, carried = run(
        step1_kernel,
        [(3 * N, N), (HALF, N)],
        *(sender_slot, with_c1, h0, out0, in0),
        scratch=JACOBI_PARTS,
    )
    in1 = onward(out1)
    with_c3 = exchange(with_c2, 1, last=(out1,))
    out2a, kept, gram2 = run(
        cross2_kernel,
        [(3 * N, HALF), (N, HALF), square],
        *(with_c2, out0, in0, out1, in1, carried),
    )
    in2a = onward(out2a)
    out2b, own2 = run(step2_kernel, [(N + HALF, HALF)] * 2, sender_slot, gram2, scratch=JACOBI_PARTS)
    in2b = onward(out2b)
    rows = matrix.shape[0]
    pair, end = run(
        columns_kernel,
        [(rows, N), (N, HALF)],
        *(out0, in0, out1, in1, own2, matrix, before1, before2),
        scratch=[pltpu.VMEM((N, 2 * N), jnp.float32)],
    )
    ends, right_cols = run(
        cross3_kernel,
        [(N + HALF, N), (rows, HALF)],
        *(out0, out1, in1, in2a, kept, own2, end, before2, before3),
        scratch=[pltpu.VMEM((N, N), jnp.float32)],
    )
    (q3,) = run(step3_kernel, [square], *(sender_slot, with_c3, ends, own2, in2b), scratch=JACOBI_PARTS)

    def last_columns(place):
        return run(functools.partial(last_kernel, place), [(rows, HALF)], pair, right_cols, in2b, q3)[0]

    arrived = onward(last_columns(HALF))
    kept = last_columns(0)
    return pl.pallas_call(
        join_kernel,
        out_shape=jax.ShapeDtypeStruct(matrix.shape, jnp.float32),
        in_specs=[pl.BlockSpec(memory_space=pltpu.VMEM)] * 2,
        out_specs=pl.BlockSpec(memory_space=pl.ANY),
        scratch_shapes=[pltpu.SemaphoreType.DMA((8,))],
        compiler_params=pltpu.CompilerParams(vmem_limit_bytes=16 * 2**20),
    )(kept, arrived)


def solution(mesh):
    return jax.shard_map(
        shards,
        mesh=mesh,
        in_specs=(P("row", "blk"), P(None, "blk")),
        out_specs=P("row", "blk"),
        check_vma=False,
    )
```

```python
import functools

import jax
import jax.numpy as jnp
from jax import lax
from jax.experimental import pallas as pl
from jax.experimental.pallas import tpu as pltpu
from jax.sharding import PartitionSpec as P

STEPS = 4
ROUNDS = 8
N = 256
HALF = 128
TILES = 64
PERIOD = N - 1


def dot(left, right, over=(1, 0), precision=lax.Precision.HIGHEST):
    return lax.dot_general(
        left,
        right,
        (((over[0],), (over[1],)), ((), ())),
        precision=precision,
        preferred_element_type=jnp.float32,
    )


def halved(values):
    high = values.astype(jnp.bfloat16)
    return high, (values - high.astype(jnp.float32)).astype(jnp.bfloat16)


def cross_dot(left, right, over=(1, 0)):
    numbers = (((over[0],), (over[1],)), ((), ()))
    (a, b), (c, d) = halved(left), halved(right)
    passes = [lax.dot_general(x, y, numbers, preferred_element_type=jnp.float32) for x, y in ((a, d), (b, c), (a, c))]
    return passes[0] + passes[1] + passes[2]


def seats(position, round_index):
    upper = position + round_index
    upper = jnp.where(upper >= PERIOD, upper - PERIOD, upper)
    lower = round_index - (position - HALF)
    lower = jnp.where(lower < 0, lower + PERIOD, lower)
    return jnp.where(position < HALF, upper, jnp.where(position == HALF, PERIOD, lower))


def placing(round_index, swapped=None):
    index = lax.broadcasted_iota(jnp.int32, (N, N), 0)
    if swapped is not None:
        index = jnp.where(swapped, jnp.where(index < HALF, index + HALF, index - HALF), index)
    position = lax.broadcasted_iota(jnp.int32, (N, N), 1)
    return (index == seats(position, round_index)).astype(jnp.bfloat16)


def thirds(values):
    high = values.astype(jnp.bfloat16)
    rest = values - high.astype(jnp.float32)
    middle = rest.astype(jnp.bfloat16)
    return high, middle, (rest - middle.astype(jnp.float32)).astype(jnp.bfloat16)


def placed(pieces, place, over):
    numbers = (((1,), (over,)), ((), ()))
    return [lax.dot_general(x, place, numbers, preferred_element_type=jnp.float32) for x in pieces]


def laid_both(values, place, over):
    columns = [x.astype(jnp.bfloat16) for x in placed(thirds(values), place, over)]
    numbers = (((over,), (0,)), ((), ()))
    return sum(lax.dot_general(place, x, numbers, preferred_element_type=jnp.float32) for x in columns)


def rotations(upper_diag, coupling, lower_diag, round_index):
    position = lax.broadcasted_iota(jnp.int32, (1, HALF), 1)
    is_lower = seats(position, round_index) < seats(position + HALF, round_index)
    difference = jnp.where(is_lower, lower_diag - upper_diag, upper_diag - lower_diag)
    x = jnp.abs(difference)
    y = jnp.where(difference >= 0.0, 2.0 * coupling, -2.0 * coupling)
    largest = jnp.maximum(x, jnp.abs(y))
    scale = jnp.where(largest > 0.0, largest, 1.0)
    inverse = 1.0 / scale
    x = jnp.where(largest > 0.0, x * inverse, 1.0)
    y = y * inverse
    tangent = y / (x + jnp.sqrt(x * x + y * y))
    cosine = 1.0 / jnp.sqrt(1.0 + tangent * tangent)
    sine = tangent * cosine
    return cosine, jnp.where(is_lower, -sine, sine)


def turn(upper, lower, cosine, sine):
    return cosine * upper + sine * lower, cosine * lower - sine * upper


def shift(upper, lower, axis):
    at = lax.broadcasted_iota(jnp.int32, upper.shape, axis)
    new_upper = jnp.where(at == HALF - 1, lower, pltpu.roll(upper, HALF - 1, axis))
    moved = pltpu.roll(jnp.where(at == 0, upper, lower), 1, axis)
    return new_upper, jnp.where(at == 0, lower, moved)


def jacobi(gram, offset, second, parts):
    uu, ul, lu, ll, qu, ql = parts
    start = placing(offset)
    laid_out = laid_both(gram, start, 0)
    uu[...] = laid_out[:HALF, :HALF]
    ul[...] = laid_out[:HALF, HALF:]
    lu[...] = laid_out[HALF:, :HALF]
    ll[...] = laid_out[HALF:, HALF:]
    qu[...] = start[:, :HALF].astype(jnp.float32)
    ql[...] = start[:, HALF:].astype(jnp.float32)
    shape = (HALF, HALF)
    eye = lax.broadcasted_iota(jnp.int32, shape, 0) == lax.broadcasted_iota(jnp.int32, shape, 1)

    def diagonal(ref):
        return jnp.sum(jnp.where(eye, ref[...], 0.0), axis=0, keepdims=True)

    def stood(row):
        return jnp.sum(jnp.where(eye, jnp.broadcast_to(row, shape), 0.0), axis=1, keepdims=True)

    for round_index in range(offset, offset + ROUNDS):
        cosine, sine = rotations(diagonal(uu), diagonal(ul), diagonal(ll), round_index)
        cosine_col, sine_col = stood(cosine), stood(sine)
        a, c = turn(uu[...], lu[...], cosine_col, sine_col)
        b, d = turn(ul[...], ll[...], cosine_col, sine_col)
        a, b = shift(*turn(a, b, cosine, sine), 1)
        c, d = shift(*turn(c, d, cosine, sine), 1)
        uu[...], lu[...] = shift(a, c, 0)
        ul[...], ll[...] = shift(b, d, 0)
        qu[...], ql[...] = shift(*turn(qu[...], ql[...], cosine, sine), 1)
    end = placing(offset + ROUNDS, second == 0)
    rotation = sum(placed(thirds(jnp.concatenate([qu[...], ql[...]], axis=1)), end, 1))
    upper = jnp.concatenate([uu[...], ul[...]], axis=1)
    lower = jnp.concatenate([lu[...], ll[...]], axis=1)
    rotated_gram = laid_both(jnp.concatenate([upper, lower], axis=0), end, 1)
    return rotation, rotated_gram


def joined(kept_gram, cross, moved_gram):
    upper = jnp.concatenate([kept_gram, cross], axis=1)
    lower = jnp.concatenate([cross.T, moved_gram], axis=1)
    return jnp.concatenate([upper, lower], axis=0)


def tiles(square):
    sides = [square[:, :HALF].reshape(-1, 1, 8, HALF), square[:, HALF:].reshape(-1, 1, 8, HALF)]
    return jnp.concatenate(sides, axis=1)


def square_of(received, place):
    count, height = received.shape[0], TILES // received.shape[0] * 8
    part = received[:, place * height : (place + 1) * height, :].reshape(TILES // 2, 2, 8, HALF)
    return jnp.concatenate([part[:, 0].reshape(N, HALF), part[:, 1].reshape(N, HALF)], axis=1)


def pack_kernel(skipped, received, *refs):
    *blocks, out = refs
    count, height = out.shape[0], TILES // out.shape[0] * 8
    if received is not None:
        spread = received.shape[1] - skipped * height
        own = jnp.sum(received[:, skipped * height :, :], axis=0, keepdims=True)
        out[:, :spread, :] = jnp.broadcast_to(own, (count, spread, HALF))
    else:
        spread = 0
    for number, block in enumerate(blocks):
        at = spread + number * height
        out[:, at : at + height, :] = tiles(block[...]).reshape(count, height, HALF)


def step0_kernel(second, received, out, h0, *parts):
    q0, rotated_gram = jacobi(square_of(received, 0), 0, second[0, 0], parts)
    h0[...] = rotated_gram[:HALF, :HALF]
    out[:N] = q0
    out[N:] = rotated_gram[HALF:]


def step1_kernel(second, received, h0, out0, in0, out, carried, *parts):
    q0_p = in0[:N]
    r1 = cross_dot(cross_dot(out0[:N], square_of(received, 1), (0, 0)), q0_p)
    out[N + HALF : 2 * N] = r1[HALF:]
    out[2 * N :] = q0_p
    carried[:, HALF:N] = r1[:HALF, :HALF]
    carried[:, N:] = in0[N:, :HALF]
    q1, h1 = jacobi(joined(h0[...], r1[:HALF, HALF:], in0[N:, HALF:]), ROUNDS, second[1, 0], parts)
    out[:N] = q1
    out[N : N + HALF] = h1[HALF:]
    carried[:, :HALF] = h1[:HALF, :HALF]


def cross2_kernel(received, out0, out1, in1, carried, out, kept, gram):
    q0_pp = in1[2 * N :]
    r2 = cross_dot(cross_dot(out0[:N], square_of(received, 0), (0, 0)), q0_pp)
    upper = jnp.concatenate([carried[:, HALF:N], r2[:HALF, HALF:]], axis=1)
    lower = jnp.concatenate([carried[:, N:], in1[N + HALF : 2 * N, HALF:]], axis=1)
    s1 = cross_dot(cross_dot(out1[:N], jnp.concatenate([upper, lower], axis=0), (0, 0)), in1[:N])
    gram[...] = joined(carried[:, :HALF], s1[:HALF, HALF:], in1[N : N + HALF, HALF:])
    out[:HALF] = s1[HALF:, HALF:]
    out[HALF:N] = r2[HALF:, HALF:]
    out[N : 2 * N] = in1[:N, HALF:]
    out[2 * N :] = q0_pp[:, HALF:]
    kept[:HALF] = s1[:HALF, :HALF]
    kept[HALF:] = r2[:HALF, :HALF]


def step2_kernel(second, gram, out, own, *parts):
    q2, h2 = jacobi(gram[...], 2 * ROUNDS, second[2, 0], parts)
    out[:N] = q2[:, HALF:]
    out[N:] = h2[HALF:, HALF:]
    own[:N] = q2[:, :HALF]
    own[N:] = h2[:HALF, :HALF]


def in_chunks(count, some_rows):
    step = min(N, count)

    def one(number, carry):
        some_rows(pl.ds(pl.multiple_of(number * step, step), step))
        return carry

    lax.fori_loop(0, count // step, one, 0)


def columns_kernel(out0, in0, out1, in1, own2, x0, x1, x2, pair, end, weights):
    q2_kk, q2_mk, q0_pp = own2[:HALF], own2[HALF:N], in1[2 * N :]
    p1_kk, p1_mk, p1_km, p1_mm = in1[:HALF, :HALF], in1[HALF:N, :HALF], in1[:HALF, HALF:], in1[HALF:N, HALF:]
    end[...] = cross_dot(out0[:N, :HALF], cross_dot(out1[:HALF, :HALF], q2_kk))
    travelled = cross_dot(in0[:N, HALF:], cross_dot(out1[HALF:N, :HALF], q2_kk))
    weights[:, :HALF] = travelled + cross_dot(in0[:N, :HALF], cross_dot(p1_km, q2_mk))
    weights[:, HALF:N] = cross_dot(in0[:N, :HALF], p1_kk)
    weights[:, N : N + HALF] = cross_dot(q0_pp[:, HALF:], cross_dot(p1_mm, q2_mk))
    weights[:, N + HALF :] = cross_dot(q0_pp[:, HALF:], p1_mk)

    def some_rows(rows):
        both = cross_dot(x1[rows, :], weights[:, :N]) + cross_dot(x2[rows, :], weights[:, N:])
        pair[rows, :HALF] = cross_dot(x0[rows, :], end[...]) + both[:, :HALF]
        pair[rows, HALF:] = both[:, HALF:]

    in_chunks(pair.shape[0], some_rows)


def cross3_kernel(out0, out1, in1, in2a, kept, own2, end, x2, x3, ends, right_cols, weights):
    q1_k, q2_k = out1[:N, :HALF], own2[:N]
    q1_pp, q0_ppp = in2a[N : 2 * N], in2a[2 * N :]
    upper = jnp.concatenate([kept[HALF:], jnp.zeros((HALF, HALF), jnp.float32)], axis=1)
    lower = jnp.concatenate([in1[N + HALF : 2 * N, :HALF], in2a[HALF:N]], axis=1)
    t = cross_dot(q1_k, cross_dot(jnp.concatenate([upper, lower], axis=0), q1_pp), (0, 0))
    upper = jnp.concatenate([kept[:HALF], t], axis=1)
    lower = jnp.concatenate([in1[N : N + HALF, :HALF], in2a[:HALF]], axis=1)
    ends[N:] = cross_dot(q2_k, jnp.concatenate([upper, lower], axis=0), (0, 0))
    weights[:, :HALF] = cross_dot(in1[2 * N :, :HALF], q1_pp[:HALF])
    weights[:, HALF:] = cross_dot(q0_ppp, q1_pp[HALF:])
    ends[:N, :HALF] = end[...]
    ends[:N, HALF:] = weights[:, HALF:]

    def some_rows(rows):
        right_cols[rows, :] = cross_dot(x2[rows, :], weights[:, :HALF]) + cross_dot(x3[rows, :], weights[:, HALF:])

    in_chunks(right_cols.shape[0], some_rows)


def last_kernel(place, pair, right_cols, in2b, q3, out):
    kept_weight, weight = q3[:HALF, place : place + HALF], q3[HALF:, place : place + HALF]
    left_weight, right_weight = cross_dot(in2b[:HALF], weight), cross_dot(in2b[HALF:N], weight)
    total = cross_dot(pair[...], jnp.concatenate([kept_weight, left_weight], axis=0))
    out[...] = total + cross_dot(right_cols[...], right_weight)


def join_kernel(kept, arrived, out, sems):
    step, copies = kept.shape[0] // 4, []
    for number in range(4):
        rows = pl.ds(number * step, step)
        for side, half in enumerate((kept, arrived)):
            target = out.at[rows, pl.ds(side * HALF, HALF)]
            copies.append(pltpu.make_async_copy(half.at[rows, :], target, sems.at[2 * number + side]))
    for copy in copies:
        copy.start()
    for copy in copies:
        copy.wait()


def step3_kernel(second, received, ends, own2, in2b, q3, *parts):
    farthest = cross_dot(square_of(received, 0), cross_dot(ends[:N, HALF:], in2b[HALF:N]))
    cross = cross_dot(ends[N:], in2b[:N]) + cross_dot(ends[:N, :HALF], farthest, (0, 0))
    gram = joined(own2[N:], cross, in2b[N:])
    q3[...], _ = jacobi(gram, 3 * ROUNDS, second[3, 0], parts)


def products_kernel(left, right, out):
    out[...] = jnp.zeros(out.shape, jnp.float32)

    def some_rows(rows):
        out[...] += cross_dot(left[rows, :], right[rows, :], (0, 0))

    in_chunks(left.shape[0], some_rows)


JACOBI_PARTS = [pltpu.VMEM((HALF, HALF), jnp.float32)] * 4 + [pltpu.VMEM((N, HALF), jnp.float32)] * 2


def run(kernel, shapes, *operands, last=(), scratch=()):
    whole, smem = pl.BlockSpec(memory_space=pltpu.VMEM), pl.BlockSpec(memory_space=pltpu.SMEM)
    specs = [smem if x.dtype == jnp.int32 else whole for x in operands]
    specs += [pl.BlockSpec(memory_space=pl.ANY)] * len(last)

    def body(*refs):
        kernel(*refs[: len(operands)], *refs[len(operands) + len(last) :])

    return pl.pallas_call(
        body,
        out_shape=[jax.ShapeDtypeStruct(shape, jnp.float32) for shape in shapes],
        in_specs=specs,
        out_specs=[whole] * len(shapes),
        scratch_shapes=scratch,
        compiler_params=pltpu.CompilerParams(vmem_limit_bytes=16 * 2**20),
        cost_estimate=pl.CostEstimate(flops=10**6, bytes_accessed=2**10, transcendentals=0),
    )(*operands, *last)


def shards(matrix, sender_slot):
    devices, count = lax.axis_size("blk"), lax.axis_size("row")

    def onward(values, places=1):
        return lax.ppermute(values, "blk", [((i - places) % devices, i) for i in range(devices)])

    def products(other):
        return run(products_kernel, [(N, N)], matrix, other)[0]

    def exchange(received, skipped, *blocks, last=()):
        height = TILES // count * 8
        given = [] if received is None else [received]
        total = len(blocks) * height + (0 if received is None else received.shape[1] - skipped * height)

        def kernel(*refs):
            pack_kernel(skipped, refs[0] if given else None, *refs[len(given) :])

        (pieces,) = run(kernel, [(count, total, HALF)], *given, *blocks, last=last)
        return lax.all_to_all(pieces, "row", 0, 0, tiled=True)

    square, block = (N, N), (HALF, HALF)
    before1, gram = lax.optimization_barrier((onward(matrix), products(matrix)))
    received = exchange(None, 0, gram, products(before1))
    before2 = onward(before1)
    with_c1 = exchange(received, 0, products(before2))
    before3 = onward(before2)
    parts3 = products(before3)
    with_c2 = exchange(with_c1, 2, parts3)
    out0, h0 = run(
        step0_kernel, [(N + HALF, N), block], sender_slot, with_c1, scratch=JACOBI_PARTS, last=(parts3,)
    )
    in0 = onward(out0)
    out1, carried = run(
        step1_kernel,
        [(3 * N, N), (HALF, N + HALF)],
        *(sender_slot, with_c1, h0, out0, in0),
        scratch=JACOBI_PARTS,
    )
    in1 = onward(out1)
    with_c3 = exchange(with_c2, 1, last=(out1,))
    out2a, kept, gram2 = run(
        cross2_kernel,
        [(3 * N, HALF), (N, HALF), square],
        *(with_c2, out0, out1, in1, carried),
    )
    in2a = onward(out2a)
    out2b, own2 = run(step2_kernel, [(N + HALF, HALF)] * 2, sender_slot, gram2, scratch=JACOBI_PARTS)
    in2b = onward(out2b)
    rows = matrix.shape[0]
    pair, end = run(
        columns_kernel,
        [(rows, N), (N, HALF)],
        *(out0, in0, out1, in1, own2, matrix, before1, before2),
        scratch=[pltpu.VMEM((N, 2 * N), jnp.float32)],
    )
    ends, right_cols = run(
        cross3_kernel,
        [(N + HALF, N), (rows, HALF)],
        *(out0, out1, in1, in2a, kept, own2, end, before2, before3),
        scratch=[pltpu.VMEM((N, N), jnp.float32)],
    )
    (q3,) = run(step3_kernel, [square], *(sender_slot, with_c3, ends, own2, in2b), scratch=JACOBI_PARTS)

    def last_columns(place):
        return run(functools.partial(last_kernel, place), [(rows, HALF)], pair, right_cols, in2b, q3)[0]

    arrived = onward(last_columns(HALF))
    kept = last_columns(0)
    return pl.pallas_call(
        join_kernel,
        out_shape=jax.ShapeDtypeStruct(matrix.shape, jnp.float32),
        in_specs=[pl.BlockSpec(memory_space=pltpu.VMEM)] * 2,
        out_specs=pl.BlockSpec(memory_space=pl.ANY),
        scratch_shapes=[pltpu.SemaphoreType.DMA((8,))],
        compiler_params=pltpu.CompilerParams(vmem_limit_bytes=16 * 2**20),
    )(kept, arrived)


def solution(mesh):
    return jax.shard_map(
        shards,
        mesh=mesh,
        in_specs=(P("row", "blk"), P(None, "blk")),
        out_specs=P("row", "blk"),
        check_vma=False,
    )
```
